128 devices in a mesh: radial: 16 (over x, y), mode: 8 (over z, core).
Axes of the slice: x: 4, y: 4, z: 4, core: 2. Of those that a mesh axis runs over, the one named last changes fastest.
Arguments:
- scalar_field: float32 [512, 128, 2, 384], P('radial', 'mode'), may hold values from -48 to 48
- radial_flow: float32 [512, 128, 2, 384], P('radial', 'mode'), may hold values from -6 to 6
- legendre: bfloat16 [128, 384, 768], P('mode'), may hold values from -0.3125 to 0.3125
- diffusivity: float32 [512], P('radial'), may hold values from 1000 to 100000
Outputs:
- field_new: float32 [512, 128, 2, 384], P('radial', 'mode')
The draws below stay inside these ranges and needn't reach their ends.
All inputs are finite; a program needn't handle non-finite values.
Results may differ from the reference program's by a relative error of at most 0.0071.
Values may be sent and summed in bfloat16 or wider, within the bound.
No kernel may reach another device: no remote copies, remote signals or barrier semaphores. Data moves between devices by JAX's collectives and lax.ppermute only.
A program may use at most 128 MiB of HBM per device.

```python
import math
import jax
import jax.numpy as jnp
from jax import lax

DEG = 384
NLAT = 768
NLON = 1536
NR = 512
ORDERS = 128
ROFF = 275


def shard_levels(key, dims, cuts, smallest, high):
    gain = 1.0
    for dim, parts in cuts:
        draws = jax.random.uniform(jax.random.fold_in(jax.random.fold_in(key, 6), dim), (parts,), jnp.float32, smallest / len(cuts), high / len(cuts))
        gain = gain * jnp.repeat(jnp.exp(draws), dims[dim] // parts).reshape((-1,) + (1,) * (len(dims) - 1 - dim))
    return gain


def normal_values(stream_key, dims, width, reach, split=(), held_as=jnp.bfloat16):
    drawn = jax.random.normal(stream_key, dims, jnp.float32) * width
    if len(split) > 0:
        drawn = shard_levels(stream_key, dims, split, -0.22, 0.18) * drawn
    return jnp.clip(drawn, min=-reach, max=reach).astype(held_as)


def setup_inputs(seed: int = 0) -> dict:
    seeds = jax.random.split(jax.random.key(seed), 5)
    return {
        "scalar_field": normal_values(seeds[0], (NR, ORDERS, 2, DEG), 8.0, 48.0, ((0, 16), (1, 8)), jnp.float32),
        "radial_flow": normal_values(seeds[1], (NR, ORDERS, 2, DEG), 1.0, 6.0, ((0, 16), (1, 8)), jnp.float32),
        "legendre": normal_values(seeds[2], (ORDERS, DEG, NLAT), DEG ** -0.5, 0.3125, ((0, 8),)),
        "diffusivity": jnp.clip(jnp.exp(math.log(100000.0) - 4.6051702 * jax.random.uniform(seeds[3], (NR,), jnp.float32) ** shard_levels(seeds[3], (NR,), ((0, 16),), -0.2, 0.2)), 1000.0, 100000.0),
    }


def longitude_tables(orders, points):
    order_ids = jnp.arange(orders, dtype=jnp.int32)
    point_ids = jnp.arange(points, dtype=jnp.int32)
    phase = order_ids[:, None] * point_ids[None, :] % points
    angle = phase.astype(jnp.float32) * (2.0 * math.pi / points)
    cosine = jnp.cos(angle)
    sine_part = jnp.sin(angle)
    paired = jnp.stack([cosine, -sine_part], axis=1)
    synth_table = (paired / math.sqrt(orders)).astype(jnp.bfloat16)
    analysis_table = (paired * math.sqrt(2.0 / points)).astype(jnp.bfloat16)
    return (synth_table, analysis_table)

def rounded(values):
    return lax.optimization_barrier(values.astype(jnp.bfloat16)).astype(jnp.float32)

def tridiagonal_solve(right_side, diffusivity):
    degree = jnp.arange(ORDERS, dtype=jnp.float32)[:, None] + jnp.arange(DEG, dtype=jnp.float32)[None, :]
    angular = degree * (degree + 1.0)
    shell_ids = jnp.arange(NR, dtype=jnp.int32)

    def forward(carry, inputs):
        ratio_prev, value_prev = carry
        kappa_shell, source, shell_index = inputs
        lower = jnp.where(shell_index > 0, -kappa_shell, 0.0)
        upper = jnp.where(shell_index < NR - 1, -kappa_shell, 0.0)
        radius = (ROFF + shell_index).astype(jnp.float32)
        diagonal = 1.0 + 2.0 * kappa_shell + kappa_shell * angular / (radius * radius)
        pivot = diagonal - lower * ratio_prev
        ratio_now = upper / pivot
        value_now = (source - lower * value_prev) / pivot[:, None, :]
        return ((ratio_now, value_now), (ratio_now, value_now))
    blank_ratio = jnp.zeros((ORDERS, DEG), jnp.float32)
    blank_value = jnp.zeros((ORDERS, 2, DEG), jnp.float32)
    _, (ratios, values) = lax.scan(forward, (blank_ratio, blank_value), (diffusivity, right_side, shell_ids))

    def backward(beyond, inputs):
        ratio_now, value_now = inputs
        solved = value_now - ratio_now[:, None, :] * beyond
        return (solved, solved)
    _, solution = lax.scan(backward, blank_value, (ratios, values), reverse=True)
    return solution

def reference(scalar_field, radial_flow, legendre, diffusivity):
    synth_table, analysis_table = longitude_tables(ORDERS, NLON)
    synth_wide = synth_table.astype(jnp.float32)
    analysis_wide = analysis_table.astype(jnp.float32)
    legendre_wide = legendre.astype(jnp.float32)

    def shell_forcing(shell_pair):
        field_shell, flow_shell = shell_pair
        field_lat = rounded(jnp.einsum('mcj,mjt->mct', rounded(field_shell), legendre_wide))
        flow_lat = rounded(jnp.einsum('mcj,mjt->mct', rounded(flow_shell), legendre_wide))
        field_grid = jnp.einsum('mct,mcp->tp', field_lat, synth_wide)
        flow_grid = jnp.einsum('mct,mcp->tp', flow_lat, synth_wide)
        product = rounded(field_grid * flow_grid)
        product_modes = rounded(jnp.einsum('tp,mcp->mct', product, analysis_wide))
        return jnp.einsum('mct,mjt->mcj', product_modes, legendre_wide)
    forcing = lax.map(shell_forcing, (scalar_field, radial_flow))
    right_side = scalar_field + forcing
    return tridiagonal_solve(right_side, diffusivity)
```

```python
import functools
import math

import jax
import jax.numpy as jnp
import ml_dtypes
import numpy as np
from jax import lax
from jax.experimental import pallas as pl
from jax.experimental.pallas import tpu as pltpu
from jax.sharding import Mesh
from jax.sharding import PartitionSpec as P

F32, BF16 = jnp.float32, jnp.bfloat16
MODE = ("mode_0", "mode_1")
RADIAL = ("radial_0", "radial_1")
NLON = 1536
POINTS = 384
LANES = 128
SHELLS, ORD, HALVES, DEG, NLAT = 32, 16, 2, 384, 768
TILES = DEG // LANES
ROWS = ORD * TILES * HALVES
LAT_TILES = NLAT // LANES
NMODE = 8
NSHELL = SHELLS // NMODE
PAIRS = ORD * HALVES
VMEM_LIMIT = 56 * 2**20


def params():
    return pltpu.CompilerParams(vmem_limit_bytes=VMEM_LIMIT)


def cost(flops, nbytes):
    return pl.CostEstimate(flops=flops, bytes_accessed=nbytes, transcendentals=0)


def whole(space=pltpu.VMEM):
    return pl.BlockSpec(memory_space=space)


def fixed(shape):
    return pl.BlockSpec(shape, lambda *_: (0,) * len(shape))


def longitude_tables(orders):
    step = NLON // POINTS
    points = np.arange(POINTS) * step
    phase = (np.arange(orders)[:, None] * points[None, :]) % NLON
    angle = phase * (2.0 * math.pi / NLON)
    paired = np.stack([np.cos(angle), -np.sin(angle)], axis=1).reshape(2 * orders, POINTS)
    synth = (paired / math.sqrt(orders)).astype(np.float32).astype(ml_dtypes.bfloat16)
    analysis = (paired * math.sqrt(2.0 / NLON)).astype(np.float32).astype(ml_dtypes.bfloat16)
    return synth.T.copy(), (analysis.astype(np.float32) * step).astype(ml_dtypes.bfloat16)


def to_rows(array):
    array = array.reshape(SHELLS, ORD, HALVES, TILES, LANES).transpose(0, 1, 3, 2, 4)
    return array.reshape(SHELLS * ROWS, LANES)


def from_rows(rows):
    rows = rows.reshape(SHELLS, ORD, TILES, HALVES, LANES).transpose(0, 1, 3, 2, 4)
    return rows.reshape(SHELLS, ORD, HALVES, DEG)


def row_of(order, tile, half):
    return (order * TILES + tile) * HALVES + half


SYNTH_ORDERS = 2


def synthesis_kernel(field, flow, legendre, out, held):
    step = pl.program_id(0)
    for k in range(SYNTH_ORDERS):
        order = step * SYNTH_ORDERS + k
        rows = []
        for source in (field, flow):
            for half in range(HALVES):
                parts = [
                    source[pl.ds(row_of(order, tile, half), SHELLS, stride=ROWS), :]
                    for tile in range(TILES)
                ]
                rows.append(jnp.concatenate(parts, axis=1))
        spectral = jnp.concatenate(rows, axis=0).astype(BF16)
        lat = jnp.dot(spectral, legendre[k], preferred_element_type=F32)
        for f in range(2):
            for half in range(HALVES):
                top = (f * HALVES + half) * SHELLS
                for tile in range(LAT_TILES):
                    held[
                        tile,
                        pl.ds(f * SHELLS * PAIRS + order * HALVES + half, SHELLS, stride=PAIRS),
                        :,
                    ] = lat[top : top + SHELLS, tile * LANES : (tile + 1) * LANES]

    @pl.when(step == ORD // SYNTH_ORDERS - 1)
    def _():
        for f in range(2):
            for dest in range(NMODE):
                for s in range(NSHELL):
                    top = (f * SHELLS + dest * NSHELL + s) * PAIRS
                    for tile in range(LAT_TILES):
                        out[dest, f, s, :, tile * LANES : (tile + 1) * LANES] = held[
                            tile, top : top + PAIRS, :
                        ].astype(BF16)


def synthesis(field_rows, flow_rows, legendre):
    shape = (NMODE, 2, NSHELL, PAIRS, NLAT)
    return pl.pallas_call(
        synthesis_kernel,
        out_shape=jax.ShapeDtypeStruct(shape, BF16),
        grid=(ORD // SYNTH_ORDERS,),
        in_specs=[
            fixed((SHELLS * ROWS, LANES)),
            fixed((SHELLS * ROWS, LANES)),
            pl.BlockSpec((SYNTH_ORDERS, DEG, NLAT), lambda i: (i, 0, 0)),
        ],
        out_specs=fixed(shape),
        scratch_shapes=[pltpu.VMEM((LAT_TILES, 2 * SHELLS * PAIRS, LANES), F32)],
        compiler_params=params(),
        cost_estimate=cost(2 * 128 * DEG * NLAT * ORD, 16_000_000),
        name="synthesis",
    )(field_rows, flow_rows, legendre)


def grid_kernel(synth, analysis, lat, out):
    field = jnp.dot(synth[...], lat[:, 0, 0].reshape(NMODE * PAIRS, NLAT), preferred_element_type=F32)
    flow = jnp.dot(synth[...], lat[:, 1, 0].reshape(NMODE * PAIRS, NLAT), preferred_element_type=F32)
    product = (field * flow).astype(BF16)
    modes = jnp.dot(analysis[...], product, preferred_element_type=F32).astype(BF16)
    out[:, 0] = modes.reshape(NMODE, PAIRS, NLAT)


def grid_product(synth, analysis, lat):
    return pl.pallas_call(
        grid_kernel,
        out_shape=jax.ShapeDtypeStruct((NMODE, NSHELL, PAIRS, NLAT), BF16),
        grid=(NSHELL,),
        in_specs=[
            fixed(synth.shape),
            fixed(analysis.shape),
            pl.BlockSpec((NMODE, 2, 1, PAIRS, NLAT), lambda i: (0, 0, i, 0, 0)),
        ],
        out_specs=pl.BlockSpec((NMODE, 1, PAIRS, NLAT), lambda i: (0, i, 0, 0)),
        compiler_params=params(),
        cost_estimate=cost(3 * 2 * POINTS * 256 * NLAT * NSHELL, 5_000_000),
        name="grid_product",
    )(synth, analysis, lat)


def block_matrix_kernel(shell, angular, pivots, left, right, ends):
    ang = angular[...]
    ratio = jnp.zeros((ROWS, LANES), F32)
    answer = jnp.ones((ROWS, LANES), F32)
    ratios = []
    for i in range(SHELLS):
        kappa, low, up, radius2 = shell[0, i], shell[1, i], shell[2, i], shell[3, i]
        diagonal = 1.0 + 2.0 * kappa + kappa * ang / radius2
        inverse = 1.0 / (diagonal - low * ratio)
        ratio = up * inverse
        answer = low * inverse * answer
        pivots[i] = inverse
        left[i] = answer
    before = left[SHELLS - 1]
    behind = ratio
    right[SHELLS - 1] = behind
    ends[2] = before
    ends[3] = behind
    for i in reversed(range(SHELLS - 1)):
        ratio = shell[2, i] * pivots[i]
        before = left[i] + ratio * before
        behind = ratio * behind
        left[i] = before
        right[i] = behind
    ends[0] = before
    ends[1] = behind


def block_matrix(shell, angular):
    big = jax.ShapeDtypeStruct((SHELLS, ROWS, LANES), F32)
    return pl.pallas_call(
        block_matrix_kernel,
        out_shape=(big, big, big, jax.ShapeDtypeStruct((4, ROWS, LANES), F32)),
        in_specs=[whole(pltpu.SMEM), whole()],
        out_specs=(whole(),) * 4,
        compiler_params=params(),
        cost_estimate=cost(10_000_000, 6_000_000),
        name="block_matrix",
    )(shell, angular)


CHAIN = 4


def chain_matrix(blocks):
    links = []
    beta = None
    for first_left, first_right, last_left, last_right in blocks:
        if beta is None:
            den = jnp.ones_like(first_left)
            beta = jnp.zeros_like(first_left)
        else:
            den = 1.0 / (1.0 - first_left * beta)
        extra = last_left * beta * den
        links.append(
            (den, den * first_left, den * first_right, extra, last_left * den, beta)
        )
        beta = last_right + extra * first_right
    alpha = None
    alphas = []
    for link in links:
        alphas.append(alpha)
        alpha = link[4] if alpha is None else link[4] * alpha
    before = None
    behind = None
    for link, start in zip(reversed(links), reversed(alphas)):
        own = link[1] if start is None else link[1] * start
        before = own if before is None else own + link[2] * before
        behind = link[2] if behind is None else link[2] * behind
    return links, (before, behind, alpha, beta)


def level_kernel(place, ends, inner, outer, held):
    supers = []
    for x in range(CHAIN):
        links, own = chain_matrix(
            [tuple(ends[x * CHAIN + k, n] for n in range(4)) for k in range(CHAIN)]
        )
        supers.append(own)
        for k in range(CHAIN):
            for n in range(6):
                held[x, k, n] = links[k][n]
    links, _ = chain_matrix(supers)
    for k in range(CHAIN):
        for n in range(6):
            outer[k, n] = links[k][n]
    inner[...] = held[place[0]]


def levels(place, ends):
    rows = 8
    shape = jax.ShapeDtypeStruct((CHAIN, 6, ROWS, LANES), F32)
    spec = pl.BlockSpec((CHAIN, 6, rows, LANES), lambda i: (0, 0, i, 0))
    return pl.pallas_call(
        level_kernel,
        out_shape=(shape, shape),
        grid=(ROWS // rows,),
        in_specs=[
            whole(pltpu.SMEM),
            pl.BlockSpec((CHAIN * CHAIN, 4, rows, LANES), lambda i: (0, 0, i, 0)),
        ],
        out_specs=(spec, spec),
        scratch_shapes=[pltpu.VMEM((CHAIN, CHAIN, 6, rows, LANES), F32)],
        compiler_params=params(),
        cost_estimate=cost(10_000_000, 8_000_000),
        name="levels",
    )(place, ends)


FORCING_ORDERS = 2


def forcing_kernel(shell, modes, legendre, field, pivots, solved, ends, held):
    step = pl.program_id(0)

    @pl.when(step == 0)
    def _():
        for s in range(SHELLS):
            for tile in range(LAT_TILES):
                held[tile, s * PAIRS : (s + 1) * PAIRS, :] = modes[
                    s // NSHELL, s % NSHELL, :, tile * LANES : (tile + 1) * LANES
                ].astype(F32)

    for k in range(FORCING_ORDERS):
        order = step * FORCING_ORDERS + k
        rows = []
        for half in range(HALVES):
            parts = [
                held[tile, pl.ds(order * HALVES + half, SHELLS, stride=PAIRS), :]
                for tile in range(LAT_TILES)
            ]
            rows.append(jnp.concatenate(parts, axis=1))
        lat = jnp.concatenate(rows, axis=0).astype(BF16)
        forcing = lax.dot_general(
            lat, legendre[k], (((1,), (1,)), ((), ())), preferred_element_type=F32
        )
        for half in range(HALVES):
            for tile in range(TILES):
                place = pl.ds(row_of(order, tile, half), SHELLS, stride=ROWS)
                solved[place, :] = (
                    field[place, :]
                    + forcing[
                        half * SHELLS : (half + 1) * SHELLS, tile * LANES : (tile + 1) * LANES
                    ]
                )

    @pl.when(step == ORD // FORCING_ORDERS - 1)
    def _():
        value = solved[0:ROWS, :] * pivots[0]
        solved[0:ROWS, :] = value
        for i in range(1, SHELLS):
            here = slice(i * ROWS, (i + 1) * ROWS)
            value = (solved[here, :] + shell[1, i] * value) * pivots[i]
            solved[here, :] = value
        ends[1] = value
        for i in reversed(range(SHELLS - 1)):
            here = slice(i * ROWS, (i + 1) * ROWS)
            value = solved[here, :] + (shell[2, i] * pivots[i]) * value
            solved[here, :] = value
        ends[0] = value


def forcing_solve(shell, modes, legendre, field_rows, pivots):
    return pl.pallas_call(
        forcing_kernel,
        out_shape=(
            jax.ShapeDtypeStruct((SHELLS * ROWS, LANES), F32),
            jax.ShapeDtypeStruct((2, ROWS, LANES), F32),
        ),
        grid=(ORD // FORCING_ORDERS,),
        in_specs=[
            whole(pltpu.SMEM),
            fixed((NMODE, NSHELL, PAIRS, NLAT)),
            pl.BlockSpec((FORCING_ORDERS, DEG, NLAT), lambda i: (i, 0, 0)),
            fixed((SHELLS * ROWS, LANES)),
            fixed((SHELLS, ROWS, LANES)),
        ],
        out_specs=(fixed((SHELLS * ROWS, LANES)), fixed((2, ROWS, LANES))),
        scratch_shapes=[pltpu.VMEM((LAT_TILES, SHELLS * PAIRS, LANES), F32)],
        compiler_params=params(),
        cost_estimate=cost(2 * 64 * DEG * NLAT * ORD, 16_000_000),
        name="forcing_solve",
    )(shell, modes, legendre, field_rows, pivots)


def chain_values(links, values, first, last):
    alphas = [first]
    for k in range(CHAIN):
        first_value, last_value = values[k]
        alpha = last_value + links(k, 3) * first_value
        if alphas[-1] is not None:
            alpha = alpha + links(k, 4) * alphas[-1]
        alphas.append(alpha)
    firsts = [None] * CHAIN + [last]
    for k in reversed(range(CHAIN)):
        value = links(k, 0) * values[k][0]
        if alphas[k] is not None:
            value = value + links(k, 1) * alphas[k]
        if firsts[k + 1] is not None:
            value = value + links(k, 2) * firsts[k + 1]
        firsts[k] = value
    return alphas, firsts


def boundary_values(links, alphas, firsts, shape):
    zero = jnp.zeros(shape, F32)
    pairs = []
    for k in range(CHAIN):
        before = zero if alphas[k] is None else alphas[k] + links(k, 5) * firsts[k]
        behind = zero if firsts[k + 1] is None else firsts[k + 1]
        pairs.append((before, behind))
    return pairs


def put_in_order(position, slots, held):
    for s, slot in enumerate(slots):
        held[lax.rem(position + CHAIN - s, CHAIN)] = slot[...]


def inner_kernel(place, links, a, b, c, d, out, held):
    put_in_order(place[1], (a, b, c, d), held)
    values = [(held[k, 0], held[k, 1]) for k in range(CHAIN)]
    alphas, firsts = chain_values(lambda k, n: links[k, n], values, None, None)
    out[0] = firsts[0]
    out[1] = alphas[CHAIN]


def inner_join(place, links, slots):
    return pl.pallas_call(
        inner_kernel,
        out_shape=jax.ShapeDtypeStruct((2, ROWS, LANES), F32),
        in_specs=[whole(pltpu.SMEM)] + [whole()] * 5,
        out_specs=whole(),
        scratch_shapes=[pltpu.VMEM((CHAIN, 2, ROWS, LANES), F32)],
        compiler_params=params(),
        cost_estimate=cost(1_000_000, 2_000_000),
        name="inner_join",
    )(place, links, *slots)


FINAL_SHELLS = 8


def final_kernel(place, inner, outer, a, b, c, d, e, f, g, h, solved, left, right, out, held, pairs, edge):
    @pl.when(pl.program_id(0) == 0)
    def _():
        shape = (ROWS, LANES)
        put_in_order(place[0], (e, f, g, h), held)
        values = [(held[k, 0], held[k, 1]) for k in range(CHAIN)]
        links = lambda k, n: outer[k, n]
        alphas, firsts = chain_values(links, values, None, None)
        for k, (before, behind) in enumerate(boundary_values(links, alphas, firsts, shape)):
            pairs[k, 0] = before
            pairs[k, 1] = behind
        first, last = pairs[place[0], 0], pairs[place[0], 1]
        put_in_order(place[1], (a, b, c, d), held)
        values = [(held[k, 0], held[k, 1]) for k in range(CHAIN)]
        links = lambda k, n: inner[k, n]
        alphas, firsts = chain_values(links, values, first, last)
        for k, (before, behind) in enumerate(boundary_values(links, alphas, firsts, shape)):
            pairs[k, 0] = before
            pairs[k, 1] = behind
        edge[...] = pairs[place[1]]

    before, behind = edge[0], edge[1]
    for i in range(FINAL_SHELLS):
        here = slice(i * ROWS, (i + 1) * ROWS)
        out[here, :] = solved[here, :] + left[i] * before + right[i] * behind


def final_join(place, inner, outer, slots, super_slots, solved, left, right):
    links = fixed((CHAIN, 6, ROWS, LANES))
    two = fixed((2, ROWS, LANES))
    rows = pl.BlockSpec((FINAL_SHELLS * ROWS, LANES), lambda i: (i, 0))
    answer = pl.BlockSpec((FINAL_SHELLS, ROWS, LANES), lambda i: (i, 0, 0))
    return pl.pallas_call(
        final_kernel,
        out_shape=jax.ShapeDtypeStruct((SHELLS * ROWS, LANES), F32),
        grid=(SHELLS // FINAL_SHELLS,),
        in_specs=[whole(pltpu.SMEM), links, links] + [two] * 8 + [rows, answer, answer],
        out_specs=rows,
        scratch_shapes=[
            pltpu.VMEM((CHAIN, 2, ROWS, LANES), F32),
            pltpu.VMEM((CHAIN, 2, ROWS, LANES), F32),
            pltpu.VMEM((2, ROWS, LANES), F32),
        ],
        compiler_params=params(),
        cost_estimate=cost(3_000_000, 9_000_000),
        name="final_join",
    )(place, inner, outer, *slots, *super_slots, solved, left, right)


def ring(array, axis):
    slots = [array]
    for step in range(1, CHAIN):
        pairs = [(i, (i + step) % CHAIN) for i in range(CHAIN)]
        slots.append(lax.ppermute(array, axis, pairs))
    return slots


def exchange(array):
    return lax.all_to_all(array, MODE, 0, 0, tiled=True)


def on_device(scalar_field, radial_flow, legendre, diffusivity):
    synth, analysis = longitude_tables(ORD * NMODE)
    field_rows, flow_rows = to_rows(scalar_field), to_rows(radial_flow)
    lat = exchange(synthesis(field_rows, flow_rows, legendre))

    nr_total = SHELLS * CHAIN * CHAIN
    place = jnp.stack([lax.axis_index(RADIAL[0]), lax.axis_index(RADIAL[1])]).astype(jnp.int32)
    shell_ids = lax.axis_index(RADIAL) * SHELLS + jnp.arange(SHELLS, dtype=jnp.int32)
    radius = (nr_total * 7 // 13 + shell_ids).astype(F32)
    shell = jnp.stack(
        [
            diffusivity,
            jnp.where(shell_ids > 0, diffusivity, 0.0),
            jnp.where(shell_ids < nr_total - 1, diffusivity, 0.0),
            radius * radius,
        ]
    )
    row = np.arange(ROWS)[:, None]
    local_degree = row // (TILES * HALVES) + row // HALVES % TILES * LANES + np.arange(LANES)[None]
    degree = (local_degree + lax.axis_index(MODE) * ORD).astype(F32)
    angular = degree * (degree + 1.0)
    pivots, left, right, ends = block_matrix(shell, angular)
    inner, outer = levels(place, lax.all_gather(ends, RADIAL))

    modes = exchange(grid_product(jnp.asarray(synth), jnp.asarray(analysis), lat))
    solved, own = forcing_solve(shell, modes, legendre, field_rows, pivots)
    slots = ring(own, RADIAL[1])
    super_slots = ring(inner_join(place, inner, slots), RADIAL[0])
    return from_rows(final_join(place, inner, outer, slots, super_slots, solved, left, right))


def solution(mesh):
    finer = Mesh(
        mesh.devices.reshape(4, 4, 4, 2), ("radial_0", "radial_1", "mode_0", "mode_1")
    )
    return jax.shard_map(
        on_device,
        mesh=finer,
        in_specs=(
            P(RADIAL, MODE, None, None),
            P(RADIAL, MODE, None, None),
            P(MODE, None, None),
            P(RADIAL),
        ),
        out_specs=P(RADIAL, MODE, None, None),
        check_vma=False,
    )
```

```python
import functools
import math

import jax
import jax.numpy as jnp
import ml_dtypes
import numpy as np
from jax import lax
from jax.experimental import pallas as pl
from jax.experimental.pallas import tpu as pltpu
from jax.sharding import Mesh
from jax.sharding import PartitionSpec as P

F32, BF16 = jnp.float32, jnp.bfloat16
MODE = ("mode_0", "mode_1")
RADIAL = ("radial_0", "radial_1")
NLON = 1536
POINTS = 384
LANES = 128
SHELLS, ORD, HALVES, DEG, NLAT = 32, 16, 2, 384, 768
TILES = DEG // LANES
ROWS = ORD * TILES * HALVES
NMODE = 8
NSHELL = SHELLS // NMODE
PAIRS = ORD * HALVES


def params(mebibytes=56):
    return pltpu.CompilerParams(vmem_limit_bytes=mebibytes * 2**20)


def cost(flops, nbytes):
    return pl.CostEstimate(flops=flops, bytes_accessed=nbytes, transcendentals=0)


def whole(space=pltpu.VMEM):
    return pl.BlockSpec(memory_space=space)


def fixed(shape):
    return pl.BlockSpec(shape, lambda *_: (0,) * len(shape))


def longitude_tables(orders):
    step = NLON // POINTS
    points = np.arange(POINTS) * step
    phase = (np.arange(orders)[:, None] * points[None, :]) % NLON
    angle = phase * (2.0 * math.pi / NLON)
    paired = np.stack([np.cos(angle), -np.sin(angle)], axis=1).reshape(2 * orders, POINTS)
    synth = (paired / math.sqrt(orders)).astype(np.float32).astype(ml_dtypes.bfloat16)
    analysis = (paired * math.sqrt(2.0 / NLON)).astype(np.float32).astype(ml_dtypes.bfloat16)
    return synth.T.copy(), (analysis.astype(np.float32) * step).astype(ml_dtypes.bfloat16)


HALF = ORD // 2
PAIRS_HALF = HALF * HALVES


def moved(device, k, back):
    z, core = device // 2, device % 2
    ahead = 1 - 2 * core
    steps, other = (
        (0, 0),
        (ahead, 0),
        (-ahead, 0),
        (ahead, 1),
        (-ahead, 1),
        (2, 0),
        (2, 1),
        (0, 1),
    )[k]
    if back and k in (1, 2):
        steps = -steps
    core = 1 - core if other else core
    return (z + steps + 4) % 4 * 2 + core


def moved_all(arrays, back):
    sent = [arrays[0]]
    for k in range(1, NMODE):
        pairs = [(d, moved(d, k, back)) for d in range(NMODE)]
        sent.append(lax.ppermute(arrays[k], MODE, pairs))
    return sent


def synthesis_kernel(half, me, field, flow, legendre, *refs):
    outs, (fields, flows, table, lat, sems, table_sems, out_sems) = refs[:NMODE], refs[NMODE:]
    orders = pl.ds(half * HALF, HALF)
    copies = [
        pltpu.make_async_copy(field.at[:, orders], fields, sems.at[0]),
        pltpu.make_async_copy(flow.at[:, orders], flows, sems.at[1]),
    ]
    tables = [
        pltpu.make_async_copy(legendre.at[half * HALF + m], table.at[m], table_sems.at[m])
        for m in range(HALF)
    ]
    for copy in copies + tables:
        copy.start()
    for copy in copies:
        copy.wait()
    for m in range(HALF):
        spectral = jnp.concatenate(
            [source[:, m].reshape(SHELLS * HALVES, DEG) for source in (fields, flows)], axis=0
        ).astype(BF16)
        tables[m].wait()
        values = jnp.dot(spectral, table[m], preferred_element_type=F32).astype(BF16)
        for f in range(2):
            mine = values[f * SHELLS * HALVES : (f + 1) * SHELLS * HALVES]
            lat[:, f, :, HALVES * m : HALVES * (m + 1), :] = mine.reshape(
                NMODE, NSHELL, HALVES, NLAT
            )
    sent = []
    for k in range(NMODE):
        source = lat.at[moved(me[0], k, False)]
        sent.append(pltpu.make_async_copy(source, outs[k], out_sems.at[k]))
        sent[-1].start()
    for copy in sent:
        copy.wait()


def synthesis(half, me, field, flow, legendre):
    shape = jax.ShapeDtypeStruct((2, NSHELL, PAIRS_HALF, NLAT), BF16)
    return pl.pallas_call(
        functools.partial(synthesis_kernel, half),
        out_shape=(shape,) * NMODE,
        in_specs=[whole(pltpu.SMEM)] + [whole(pl.ANY)] * 3,
        out_specs=(whole(pl.ANY),) * NMODE,
        scratch_shapes=[
            pltpu.VMEM((SHELLS, HALF, HALVES, DEG), F32),
            pltpu.VMEM((SHELLS, HALF, HALVES, DEG), F32),
            pltpu.VMEM((HALF, DEG, NLAT), BF16),
            pltpu.VMEM((NMODE, 2, NSHELL, PAIRS_HALF, NLAT), BF16),
            pltpu.SemaphoreType.DMA((2,)),
            pltpu.SemaphoreType.DMA((HALF,)),
            pltpu.SemaphoreType.DMA((NMODE,)),
        ],
        compiler_params=params(),
        cost_estimate=cost(2 * 128 * DEG * NLAT * HALF, 8_000_000),
        name="synthesis",
    )(me, field, flow, legendre)


def grid_kernel(me, synth, analysis, *refs):
    firsts, seconds = refs[:NMODE], refs[NMODE : 2 * NMODE]
    outs = refs[2 * NMODE : 3 * NMODE]
    lat, modes, sems, out_sems = refs[3 * NMODE :]
    arrived = []
    for k in range(NMODE):
        top = moved(me[0], k, True) * PAIRS
        for h, source in enumerate((firsts[k], seconds[k])):
            place = lat.at[:, :, pl.ds(pl.multiple_of(top + h * PAIRS_HALF, PAIRS_HALF), PAIRS_HALF)]
            arrived.append(pltpu.make_async_copy(source, place, sems.at[k, h]))
            arrived[-1].start()
    for copy in arrived:
        copy.wait()
    sent = []
    for r in range(NSHELL):
        field = jnp.dot(synth[...], lat[0, r], preferred_element_type=F32)
        flow = jnp.dot(synth[...], lat[1, r], preferred_element_type=F32)
        product = (field * flow).astype(BF16)
        found = jnp.dot(analysis[...], product, preferred_element_type=F32).astype(BF16)
        modes[:, r] = found.reshape(NMODE, PAIRS, NLAT)
        for k in range(NMODE):
            source = modes.at[moved(me[0], k, True), r]
            sent.append(pltpu.make_async_copy(source, outs[k].at[r], out_sems.at[r, k]))
            sent[-1].start()
    for copy in sent:
        copy.wait()


def grid_product(me, synth, analysis, firsts, seconds):
    shape = jax.ShapeDtypeStruct((NSHELL, PAIRS, NLAT), BF16)
    return pl.pallas_call(
        grid_kernel,
        out_shape=(shape,) * NMODE,
        in_specs=[whole(pltpu.SMEM), whole(), whole()] + [whole(pl.ANY)] * (2 * NMODE),
        out_specs=(whole(pl.ANY),) * NMODE,
        scratch_shapes=[
            pltpu.VMEM((2, NSHELL, NMODE * PAIRS, NLAT), BF16),
            pltpu.VMEM((NMODE, NSHELL, PAIRS, NLAT), BF16),
            pltpu.SemaphoreType.DMA((NMODE, 2)),
            pltpu.SemaphoreType.DMA((NSHELL, NMODE)),
        ],
        compiler_params=params(16),
        cost_estimate=cost(3 * 2 * POINTS * 256 * NLAT * NSHELL, 5_000_000),
        name="grid_product",
    )(me, synth, analysis, *firsts, *seconds)


def block_matrix_kernel(shell, angular, pivots, left, right, ends):
    ang = angular[...]
    ratio = jnp.zeros((ROWS, LANES), F32)
    answer = jnp.ones((ROWS, LANES), F32)
    ratios = []
    for i in range(SHELLS):
        kappa, low, up, radius2 = shell[0, i], shell[1, i], shell[2, i], shell[3, i]
        diagonal = 1.0 + 2.0 * kappa + kappa * ang / radius2
        inverse = 1.0 / (diagonal - low * ratio)
        ratio = up * inverse
        answer = low * inverse * answer
        pivots[i] = inverse
        left[i] = answer
    before = left[SHELLS - 1]
    behind = ratio
    right[SHELLS - 1] = behind
    ends[2] = before
    ends[3] = behind
    for i in reversed(range(SHELLS - 1)):
        ratio = shell[2, i] * pivots[i]
        before = left[i] + ratio * before
        behind = ratio * behind
        left[i] = before
        right[i] = behind
    ends[0] = before
    ends[1] = behind


def block_matrix(shell, angular):
    big = jax.ShapeDtypeStruct((SHELLS, ROWS, LANES), F32)
    return pl.pallas_call(
        block_matrix_kernel,
        out_shape=(big, big, big, jax.ShapeDtypeStruct((4, ROWS, LANES), F32)),
        in_specs=[whole(pltpu.SMEM), whole()],
        out_specs=(whole(),) * 4,
        compiler_params=params(16),
        cost_estimate=cost(10_000_000, 6_000_000),
        name="block_matrix",
    )(shell, angular)


CHAIN = 4


def chain_matrix(blocks):
    links = []
    beta = None
    for first_left, first_right, last_left, last_right in blocks:
        if beta is None:
            den = jnp.ones_like(first_left)
            beta = jnp.zeros_like(first_left)
        else:
            den = 1.0 / (1.0 - first_left * beta)
        extra = last_left * beta * den
        links.append(
            (den, den * first_left, den * first_right, extra, last_left * den, beta)
        )
        beta = last_right + extra * first_right
    alpha = None
    alphas = []
    for link in links:
        alphas.append(alpha)
        alpha = link[4] if alpha is None else link[4] * alpha
    before = None
    behind = None
    for link, start in zip(reversed(links), reversed(alphas)):
        own = link[1] if start is None else link[1] * start
        before = own if before is None else own + link[2] * before
        behind = link[2] if behind is None else link[2] * behind
    return links, (before, behind, alpha, beta)


def level_kernel(place, ends, inner, outer, held):
    supers = []
    for x in range(CHAIN):
        links, own = chain_matrix(
            [tuple(ends[x * CHAIN + k, n] for n in range(4)) for k in range(CHAIN)]
        )
        supers.append(own)
        for k in range(CHAIN):
            for n in range(6):
                held[x, k, n] = links[k][n]
    links, _ = chain_matrix(supers)
    for k in range(CHAIN):
        for n in range(6):
            outer[k, n] = links[k][n]
    inner[...] = held[place[0]]


def levels(place, ends):
    rows = 8
    shape = jax.ShapeDtypeStruct((CHAIN, 6, ROWS, LANES), F32)
    spec = pl.BlockSpec((CHAIN, 6, rows, LANES), lambda i: (0, 0, i, 0))
    return pl.pallas_call(
        level_kernel,
        out_shape=(shape, shape),
        grid=(ROWS // rows,),
        in_specs=[
            whole(pltpu.SMEM),
            pl.BlockSpec((CHAIN * CHAIN, 4, rows, LANES), lambda i: (0, 0, i, 0)),
        ],
        out_specs=(spec, spec),
        scratch_shapes=[pltpu.VMEM((CHAIN, CHAIN, 6, rows, LANES), F32)],
        compiler_params=params(12),
        cost_estimate=cost(10_000_000, 8_000_000),
        name="levels",
    )(place, ends)


def forcing_kernel(me, shell, field, pivots, legendre, *refs):
    slots = refs[:NMODE]
    solved, ends, modes, sems = refs[NMODE:]
    copies = [
        pltpu.make_async_copy(
            slots[k], modes.at[pl.ds(moved(me[0], k, False) * NSHELL, NSHELL)], sems.at[k]
        )
        for k in range(NMODE)
    ]
    for copy in copies:
        copy.start()
    for copy in copies:
        copy.wait()
    for m in range(ORD):
        lat = modes[:, HALVES * m : HALVES * (m + 1), :].reshape(SHELLS * HALVES, NLAT)
        forcing = lax.dot_general(
            lat, legendre[m], (((1,), (1,)), ((), ())), preferred_element_type=F32
        )
        right_side = field[:, m].reshape(SHELLS * HALVES, DEG) + forcing
        for tile in range(TILES):
            row = (m * TILES + tile) * HALVES
            solved[:, row : row + HALVES, :] = right_side[
                :, tile * LANES : (tile + 1) * LANES
            ].reshape(SHELLS, HALVES, LANES)
    value = solved[0] * pivots[0]
    solved[0] = value
    for i in range(1, SHELLS):
        value = (solved[i] + shell[1, i] * value) * pivots[i]
        solved[i] = value
    ends[1] = value.astype(BF16)
    for i in reversed(range(SHELLS - 1)):
        value = solved[i] + (shell[2, i] * pivots[i]) * value
        solved[i] = value
    ends[0] = value.astype(BF16)


def forcing_solve(me, shell, slots, legendre, field, pivots):
    return pl.pallas_call(
        forcing_kernel,
        out_shape=(
            jax.ShapeDtypeStruct((SHELLS, ROWS, LANES), F32),
            jax.ShapeDtypeStruct((2, ROWS, LANES), BF16),
        ),
        in_specs=[whole(pltpu.SMEM)] * 2 + [whole()] * 3 + [whole(pl.ANY)] * NMODE,
        out_specs=(whole(), whole()),
        scratch_shapes=[
            pltpu.VMEM((SHELLS, PAIRS, NLAT), BF16),
            pltpu.SemaphoreType.DMA((NMODE,)),
        ],
        compiler_params=params(24),
        cost_estimate=cost(2 * 64 * DEG * NLAT * ORD, 16_000_000),
        name="forcing_solve",
    )(me, shell, field, pivots, legendre, *slots)


def chain_values(links, values, first, last):
    alphas = [first]
    for k in range(CHAIN):
        first_value, last_value = values[k]
        alpha = last_value + links(k, 3) * first_value
        if alphas[-1] is not None:
            alpha = alpha + links(k, 4) * alphas[-1]
        alphas.append(alpha)
    firsts = [None] * CHAIN + [last]
    for k in reversed(range(CHAIN)):
        value = links(k, 0) * values[k][0]
        if alphas[k] is not None:
            value = value + links(k, 1) * alphas[k]
        if firsts[k + 1] is not None:
            value = value + links(k, 2) * firsts[k + 1]
        firsts[k] = value
    return alphas, firsts


def boundary_values(links, alphas, firsts, shape):
    zero = jnp.zeros(shape, F32)
    pairs = []
    for k in range(CHAIN):
        before = zero if alphas[k] is None else alphas[k] + links(k, 5) * firsts[k]
        behind = zero if firsts[k + 1] is None else firsts[k + 1]
        pairs.append((before, behind))
    return pairs


def slot_copies(position, slots, held, sems):
    return [
        pltpu.make_async_copy(slot, held.at[lax.rem(position + CHAIN - s, CHAIN)], sems.at[s])
        for s, slot in enumerate(slots)
    ]


def inner_kernel(place, links, a, b, c, d, out, held, coefficients, sems):
    copies = slot_copies(place[1], (a, b, c, d), held, sems)
    copies.append(pltpu.make_async_copy(links, coefficients, sems.at[CHAIN]))
    for copy in copies:
        copy.start()
    for copy in copies:
        copy.wait()
    values = [(held[k, 0].astype(F32), held[k, 1].astype(F32)) for k in range(CHAIN)]
    alphas, firsts = chain_values(lambda k, n: coefficients[k, n], values, None, None)
    out[0] = firsts[0].astype(BF16)
    out[1] = alphas[CHAIN].astype(BF16)


def inner_join(place, links, slots):
    return pl.pallas_call(
        inner_kernel,
        out_shape=jax.ShapeDtypeStruct((2, ROWS, LANES), BF16),
        in_specs=[whole(pltpu.SMEM)] + [whole(pl.ANY)] * 5,
        out_specs=whole(),
        scratch_shapes=[
            pltpu.VMEM((CHAIN, 2, ROWS, LANES), BF16),
            pltpu.VMEM((CHAIN, 6, ROWS, LANES), F32),
            pltpu.SemaphoreType.DMA((CHAIN + 1,)),
        ],
        compiler_params=params(12),
        cost_estimate=cost(1_000_000, 2_000_000),
        name="inner_join",
    )(place, links, *slots)


PIECES = 4
PIECE = SHELLS // PIECES


def final_kernel(place, inner, outer, a, b, c, d, e, f, g, h, solved, left, right, out, *scratch):
    near, far, near_links, far_links, pairs, terms, result, sems, term_sems, out_sems = scratch
    copies = slot_copies(place[0], (e, f, g, h), far, sems.at[0])
    copies.append(pltpu.make_async_copy(outer, far_links, sems.at[0, CHAIN]))
    copies += slot_copies(place[1], (a, b, c, d), near, sems.at[1])
    copies.append(pltpu.make_async_copy(inner, near_links, sems.at[1, CHAIN]))
    term_copies = [
        pltpu.make_async_copy(source, terms.at[n], term_sems.at[n])
        for n, source in enumerate((solved, left, right))
    ]
    for copy in copies + term_copies:
        copy.start()
    for copy in copies:
        copy.wait()
    first = last = None
    for level, (held, links) in enumerate(((far, far_links), (near, near_links))):
        values = [(held[k, 0].astype(F32), held[k, 1].astype(F32)) for k in range(CHAIN)]
        read = lambda k, n, links=links: links[k, n]
        alphas, firsts = chain_values(read, values, first, last)
        found = boundary_values(read, alphas, firsts, (ROWS, LANES))
        for k, (before, behind) in enumerate(found):
            pairs[k, 0] = before
            pairs[k, 1] = behind
        first, last = pairs[place[level], 0], pairs[place[level], 1]
    for copy in term_copies:
        copy.wait()
    sent = []
    for piece in range(PIECES):
        for i in range(piece * PIECE, (piece + 1) * PIECE):
            value = terms[0, i] + terms[1, i] * first + terms[2, i] * last
            value = value.reshape(ORD, TILES, HALVES, LANES)
            for tile in range(TILES):
                result[i, :, :, tile * LANES : (tile + 1) * LANES] = value[:, tile]
        here = pl.ds(piece * PIECE, PIECE)
        sent.append(pltpu.make_async_copy(result.at[here], out.at[here], out_sems.at[piece]))
        sent[-1].start()
    for copy in sent:
        copy.wait()


def final_join(place, inner, outer, slots, super_slots, solved, left, right):
    return pl.pallas_call(
        final_kernel,
        out_shape=jax.ShapeDtypeStruct((SHELLS, ORD, HALVES, DEG), F32),
        in_specs=[whole(pltpu.SMEM)] + [whole(pl.ANY)] * 13,
        out_specs=whole(pl.ANY),
        scratch_shapes=[
            pltpu.VMEM((CHAIN, 2, ROWS, LANES), BF16),
            pltpu.VMEM((CHAIN, 2, ROWS, LANES), BF16),
            pltpu.VMEM((CHAIN, 6, ROWS, LANES), F32),
            pltpu.VMEM((CHAIN, 6, ROWS, LANES), F32),
            pltpu.VMEM((CHAIN, 2, ROWS, LANES), F32),
            pltpu.VMEM((3, SHELLS, ROWS, LANES), F32),
            pltpu.VMEM((SHELLS, ORD, HALVES, DEG), F32),
            pltpu.SemaphoreType.DMA((2, CHAIN + 1)),
            pltpu.SemaphoreType.DMA((3,)),
            pltpu.SemaphoreType.DMA((PIECES,)),
        ],
        compiler_params=params(24),
        cost_estimate=cost(3_000_000, 9_000_000),
        name="final_join",
    )(place, inner, outer, *slots, *super_slots, solved, left, right)


def shifted(array, axis, step):
    size = lax.axis_size(axis)
    return lax.ppermute(array, axis, [(i, (i + step) % size) for i in range(size)])


def ring(array, axis):
    return [array] + [shifted(array, axis, step) for step in range(1, CHAIN)]


def on_device(scalar_field, radial_flow, legendre, diffusivity):
    synth, analysis = (jnp.asarray(table) for table in longitude_tables(ORD * NMODE))
    mode = lax.axis_index(MODE).astype(jnp.int32)
    me = mode.reshape(1)
    firsts = list(synthesis(0, me, scalar_field, radial_flow, legendre))
    later, firsts[0] = lax.optimization_barrier((me, firsts[0]))
    seconds = synthesis(1, later, scalar_field, radial_flow, legendre)
    firsts, seconds = moved_all(firsts, False), moved_all(seconds, False)
    diffusivity, mode, firsts[7] = lax.optimization_barrier((diffusivity, mode, firsts[7]))

    nr_total = SHELLS * CHAIN * CHAIN
    place = jnp.stack([lax.axis_index(RADIAL[0]), lax.axis_index(RADIAL[1])]).astype(jnp.int32)
    shell_ids = lax.axis_index(RADIAL) * SHELLS + jnp.arange(SHELLS, dtype=jnp.int32)
    radius = (nr_total * 7 // 13 + shell_ids).astype(F32)
    shell = jnp.stack(
        [
            diffusivity,
            jnp.where(shell_ids > 0, diffusivity, 0.0),
            jnp.where(shell_ids < nr_total - 1, diffusivity, 0.0),
            radius * radius,
        ]
    )
    row = np.arange(ROWS)[:, None]
    local_degree = row // (TILES * HALVES) + row // HALVES % TILES * LANES + np.arange(LANES)[None]
    degree = (local_degree + mode * ORD).astype(F32)
    angular = degree * (degree + 1.0)
    pivots, left, right, ends = block_matrix(shell, angular)
    inner, outer = levels(place, lax.all_gather(ends, RADIAL))

    modes = moved_all(grid_product(me, synth, analysis, firsts, seconds), True)
    pivots, inner, outer = lax.optimization_barrier((pivots, inner, outer))
    solved, own = forcing_solve(me, shell, modes, legendre, scalar_field, pivots)
    slots = ring(own, RADIAL[1])
    super_slots = ring(inner_join(place, inner, slots), RADIAL[0])
    return final_join(place, inner, outer, slots, super_slots, solved, left, right)


def solution(mesh):
    finer = Mesh(
        mesh.devices.reshape(4, 4, 4, 2), ("radial_0", "radial_1", "mode_0", "mode_1")
    )
    return jax.shard_map(
        on_device,
        mesh=finer,
        in_specs=(
            P(RADIAL, MODE, None, None),
            P(RADIAL, MODE, None, None),
            P(MODE, None, None),
            P(RADIAL),
        ),
        out_specs=P(RADIAL, MODE, None, None),
        check_vma=False,
    )
```

```python
import functools
import math

import jax
import jax.numpy as jnp
import ml_dtypes
import numpy as np
from jax import lax
from jax.experimental import pallas as pl
from jax.experimental.pallas import tpu as pltpu
from jax.sharding import Mesh
from jax.sharding import PartitionSpec as P

F32, BF16 = jnp.float32, jnp.bfloat16
MODE = ("mode_0", "mode_1")
RADIAL = ("radial_0", "radial_1")
NLON = 1536
POINTS = 384
LANES = 128
SHELLS, ORD, HALVES, DEG, NLAT = 32, 16, 2, 384, 768
TILES = DEG // LANES
ROWS = ORD * TILES * HALVES
NMODE = 8
NSHELL = SHELLS // NMODE
PAIRS = ORD * HALVES


def params(mebibytes=56):
    return pltpu.CompilerParams(vmem_limit_bytes=mebibytes * 2**20)


def cost(flops, nbytes):
    return pl.CostEstimate(flops=flops, bytes_accessed=nbytes, transcendentals=0)


def whole(space=pltpu.VMEM):
    return pl.BlockSpec(memory_space=space)


def fixed(shape):
    return pl.BlockSpec(shape, lambda *_: (0,) * len(shape))


def longitude_tables(orders):
    step = NLON // POINTS
    points = np.arange(POINTS) * step
    phase = (np.arange(orders)[:, None] * points[None, :]) % NLON
    angle = phase * (2.0 * math.pi / NLON)
    paired = np.stack([np.cos(angle), -np.sin(angle)], axis=1).reshape(2 * orders, POINTS)
    synth = (paired / math.sqrt(orders)).astype(np.float32).astype(ml_dtypes.bfloat16)
    analysis = (paired * math.sqrt(2.0 / NLON)).astype(np.float32).astype(ml_dtypes.bfloat16)
    return synth.T.copy(), (analysis.astype(np.float32) * step).astype(ml_dtypes.bfloat16)


def row_of(order, tile, half):
    return (order * TILES + tile) * HALVES + half


HALF = ORD // 2
PAIRS_HALF = HALF * HALVES
AHEAD = 7


def moved(device, k, back):
    z, core = device // 2, device % 2
    ahead = 1 - 2 * core
    steps, other = (
        (0, 0),
        (ahead, 0),
        (-ahead, 0),
        (ahead, 1),
        (-ahead, 1),
        (2, 0),
        (2, 1),
        (0, 1),
    )[k]
    if back and k in (1, 2):
        steps = -steps
    core = 1 - core if other else core
    return (z + steps + 4) % 4 * 2 + core


def moved_all(arrays, back):
    sent = [arrays[0]]
    for k in range(1, NMODE):
        pairs = [(d, moved(d, k, back)) for d in range(NMODE)]
        sent.append(lax.ppermute(arrays[k], MODE, pairs))
    return sent


def synthesis_kernel(half, me, field, flow, legendre, *refs):
    outs, (fields, flows, table, lat, sems, table_sems, out_sems) = refs[:NMODE], refs[NMODE:]
    orders = pl.ds(half * HALF, HALF)
    copies = [
        pltpu.make_async_copy(field.at[:, orders], fields, sems.at[0]),
        pltpu.make_async_copy(flow.at[:, orders], flows, sems.at[1]),
    ]
    tables = [
        pltpu.make_async_copy(legendre.at[half * HALF + m], table.at[m], table_sems.at[m])
        for m in range(HALF)
    ]
    for copy in copies + tables[:AHEAD]:
        copy.start()
    for copy in copies:
        copy.wait()
    for m in range(HALF):
        if m + AHEAD < HALF:
            tables[m + AHEAD].start()
        spectral = jnp.concatenate(
            [source[:, m].reshape(SHELLS * HALVES, DEG) for source in (fields, flows)], axis=0
        ).astype(BF16)
        tables[m].wait()
        values = jnp.dot(spectral, table[m], preferred_element_type=F32).astype(BF16)
        for f in range(2):
            mine = values[f * SHELLS * HALVES : (f + 1) * SHELLS * HALVES]
            lat[:, f, :, HALVES * m : HALVES * (m + 1), :] = mine.reshape(
                NMODE, NSHELL, HALVES, NLAT
            )
    sent = []
    for k in range(NMODE):
        source = lat.at[moved(me[0], k, False)]
        sent.append(pltpu.make_async_copy(source, outs[k], out_sems.at[k]))
        sent[-1].start()
    for copy in sent:
        copy.wait()


def synthesis(half, me, field, flow, legendre):
    shape = jax.ShapeDtypeStruct((2, NSHELL, PAIRS_HALF, NLAT), BF16)
    return pl.pallas_call(
        functools.partial(synthesis_kernel, half),
        out_shape=(shape,) * NMODE,
        in_specs=[whole(pltpu.SMEM)] + [whole(pl.ANY)] * 3,
        out_specs=(whole(pl.ANY),) * NMODE,
        scratch_shapes=[
            pltpu.VMEM((SHELLS, HALF, HALVES, DEG), F32),
            pltpu.VMEM((SHELLS, HALF, HALVES, DEG), F32),
            pltpu.VMEM((HALF, DEG, NLAT), BF16),
            pltpu.VMEM((NMODE, 2, NSHELL, PAIRS_HALF, NLAT), BF16),
            pltpu.SemaphoreType.DMA((2,)),
            pltpu.SemaphoreType.DMA((HALF,)),
            pltpu.SemaphoreType.DMA((NMODE,)),
        ],
        compiler_params=params(58),
        cost_estimate=cost(2 * 128 * DEG * NLAT * HALF, 8_000_000),
        name="synthesis",
    )(me, field, flow, legendre)


def grid_kernel(me, synth, analysis, *refs):
    firsts, seconds = refs[:NMODE], refs[NMODE : 2 * NMODE]
    outs = refs[2 * NMODE : 3 * NMODE]
    lat, modes, sems, out_sems = refs[3 * NMODE :]
    arrived = []
    for k in range(NMODE):
        top = moved(me[0], k, True) * PAIRS
        for h, source in enumerate((firsts[k], seconds[k])):
            place = lat.at[:, :, pl.ds(pl.multiple_of(top + h * PAIRS_HALF, PAIRS_HALF), PAIRS_HALF)]
            arrived.append(pltpu.make_async_copy(source, place, sems.at[k, h]))
            arrived[-1].start()
    for copy in arrived:
        copy.wait()
    sent = []
    for r in range(NSHELL):
        field = jnp.dot(synth[...], lat[0, r], preferred_element_type=F32)
        flow = jnp.dot(synth[...], lat[1, r], preferred_element_type=F32)
        product = (field * flow).astype(BF16)
        found = jnp.dot(analysis[...], product, preferred_element_type=F32).astype(BF16)
        modes[:, r] = found.reshape(NMODE, PAIRS, NLAT)
        for k in range(NMODE):
            source = modes.at[moved(me[0], k, True), r]
            sent.append(pltpu.make_async_copy(source, outs[k].at[r], out_sems.at[r, k]))
            sent[-1].start()
    for copy in sent:
        copy.wait()


def grid_product(me, synth, analysis, firsts, seconds):
    shape = jax.ShapeDtypeStruct((NSHELL, PAIRS, NLAT), BF16)
    return pl.pallas_call(
        grid_kernel,
        out_shape=(shape,) * NMODE,
        in_specs=[whole(pltpu.SMEM), whole(), whole()] + [whole(pl.ANY)] * (2 * NMODE),
        out_specs=(whole(pl.ANY),) * NMODE,
        scratch_shapes=[
            pltpu.VMEM((2, NSHELL, NMODE * PAIRS, NLAT), BF16),
            pltpu.VMEM((NMODE, NSHELL, PAIRS, NLAT), BF16),
            pltpu.SemaphoreType.DMA((NMODE, 2)),
            pltpu.SemaphoreType.DMA((NSHELL, NMODE)),
        ],
        compiler_params=params(58),
        cost_estimate=cost(3 * 2 * POINTS * 256 * NLAT * NSHELL, 5_000_000),
        name="grid_product",
    )(me, synth, analysis, *firsts, *seconds)


def block_matrix_kernel(shell, angular, pivots, left, right):
    ang = angular[...]
    ratio = jnp.zeros((ROWS, LANES), F32)
    answer = jnp.ones((ROWS, LANES), F32)
    ratios = []
    for i in range(SHELLS):
        kappa, low, up, radius2 = shell[0, i], shell[1, i], shell[2, i], shell[3, i]
        diagonal = 1.0 + 2.0 * kappa + kappa * ang / radius2
        inverse = 1.0 / (diagonal - low * ratio)
        ratio = up * inverse
        answer = low * inverse * answer
        pivots[i] = inverse
        left[i] = answer
    before = left[SHELLS - 1]
    behind = ratio
    right[SHELLS - 1] = behind
    for i in reversed(range(SHELLS - 1)):
        ratio = shell[2, i] * pivots[i]
        before = left[i] + ratio * before
        behind = ratio * behind
        left[i] = before
        right[i] = behind


def block_matrix(shell, angular):
    big = jax.ShapeDtypeStruct((SHELLS, ROWS, LANES), F32)
    return pl.pallas_call(
        block_matrix_kernel,
        out_shape=(big, big, big),
        in_specs=[whole(pltpu.SMEM), whole()],
        out_specs=(whole(),) * 3,
        compiler_params=params(16),
        cost_estimate=cost(10_000_000, 6_000_000),
        name="block_matrix",
    )(shell, angular)


CHAIN = 4


def chain_matrix(blocks):
    links = []
    beta = None
    for first_left, first_right, last_left, last_right in blocks:
        if beta is None:
            den = jnp.ones_like(first_left)
            beta = jnp.zeros_like(first_left)
        else:
            den = 1.0 / (1.0 - first_left * beta)
        extra = last_left * beta * den
        links.append(
            (den, den * first_left, den * first_right, extra, last_left * den, beta)
        )
        beta = last_right + extra * first_right
    alpha = None
    alphas = []
    for link in links:
        alphas.append(alpha)
        alpha = link[4] if alpha is None else link[4] * alpha
    before = None
    behind = None
    for link, start in zip(reversed(links), reversed(alphas)):
        own = link[1] if start is None else link[1] * start
        before = own if before is None else own + link[2] * before
        behind = link[2] if behind is None else link[2] * behind
    return links, (before, behind, alpha, beta)


DEGREES = 512
LINKS = 6


def level_kernel(where, diffusivity, inner, outer, ordered, factors, links_held, table):
    x, y, mode = where[0], where[1], where[2]
    for k in range(CHAIN):
        for first in range(8):
            slot = lax.rem(x + CHAIN - first % CHAIN, CHAIN) * CHAIN + lax.rem(y + CHAIN - k, CHAIN)
            ordered[k, first : first + 1, :] = diffusivity[pl.ds(slot, 1), :]
    degree = lax.broadcasted_iota(jnp.int32, (1, 1, DEGREES), 2).astype(F32)
    angular = degree * (degree + 1.0)
    shape = (CHAIN, 8, 1)
    block = lax.broadcasted_iota(jnp.int32, shape, 1) % CHAIN * CHAIN
    block = block + lax.broadcasted_iota(jnp.int32, shape, 0)
    total = CHAIN * CHAIN * SHELLS

    def kappas(i):
        kappa = ordered[:, :, i : i + 1]
        low, up = kappa, kappa
        if i == 0:
            low = jnp.where(block == 0, 0.0, kappa)
        if i == SHELLS - 1:
            up = jnp.where(block == CHAIN * CHAIN - 1, 0.0, kappa)
        return kappa, low, up

    ratio = jnp.zeros((CHAIN, 8, DEGREES), F32)
    answer = jnp.ones((CHAIN, 8, DEGREES), F32)
    for i in range(SHELLS):
        kappa, low, up = kappas(i)
        radius = (total * 7 // 13 + block * SHELLS + i).astype(F32)
        diagonal = 1.0 + 2.0 * kappa + kappa * angular / (radius * radius)
        inverse = 1.0 / (diagonal - low * ratio)
        ratio = up * inverse
        answer = low * inverse * answer
        factors[0, i] = ratio
        factors[1, i] = answer
    before, behind = answer, ratio
    last_left, last_right = before, behind
    for i in reversed(range(SHELLS - 1)):
        before = factors[1, i] + factors[0, i] * before
        behind = factors[0, i] * behind
    ends = (before, behind, last_left, last_right)
    links, supers = chain_matrix([tuple(end[k] for end in ends) for k in range(CHAIN)])
    for k in range(CHAIN):
        for n in range(LINKS):
            links_held[k * LINKS + n] = links[k][n]
    far, _ = chain_matrix([tuple(end[k : k + 1] for end in supers) for k in range(CHAIN)])
    for k in range(CHAIN):
        for n in range(LINKS):
            row = k * LINKS + n
            table[row : row + 1, :] = links_held[row, pl.ds(x, 1), :]
            row_far = CHAIN * LINKS + row
            table[row_far : row_far + 1, :] = far[k][n]
    values = table[...]
    count = CHAIN * LINKS
    for m in range(ORD):
        here = pltpu.roll(values, DEGREES - (mode * ORD + m), 1)
        for tile in range(TILES):
            found = here[:, tile * LANES : (tile + 1) * LANES]
            for half in range(HALVES):
                rows = pl.ds(row_of(m, tile, half), count, stride=ROWS)
                inner[rows, :] = found[:count]
                outer[rows, :] = found[count:]


def levels(where, diffusivity):
    count = CHAIN * LINKS
    shape = jax.ShapeDtypeStruct((count * ROWS, LANES), F32)
    outs = pl.pallas_call(
        level_kernel,
        out_shape=(shape, shape),
        in_specs=[whole(pltpu.SMEM), whole()],
        out_specs=(whole(), whole()),
        scratch_shapes=[
            pltpu.VMEM((CHAIN, 8, SHELLS), F32),
            pltpu.VMEM((2, SHELLS, CHAIN, 8, DEGREES), F32),
            pltpu.VMEM((count, 8, DEGREES), F32),
            pltpu.VMEM((2 * count, DEGREES), F32),
        ],
        compiler_params=params(20),
        cost_estimate=cost(10_000_000, 8_000_000),
        name="levels",
    )(where, diffusivity)
    return [out.reshape(CHAIN, LINKS, ROWS, LANES) for out in outs]


def forcing_kernel(me, shell, field, pivots, legendre, *refs):
    slots = refs[:NMODE]
    solved, ends, modes, table, fields, inverses, sems, table_sems = refs[NMODE:]
    copies = [
        pltpu.make_async_copy(
            slots[k], modes.at[pl.ds(moved(me[0], k, False) * NSHELL, NSHELL)], sems.at[k]
        )
        for k in range(NMODE)
    ]
    copies.append(pltpu.make_async_copy(field, fields, sems.at[NMODE]))
    last = pltpu.make_async_copy(pivots, inverses, sems.at[NMODE + 1])
    tables = [
        pltpu.make_async_copy(legendre.at[m], table.at[m], table_sems.at[m]) for m in range(ORD)
    ]
    for copy in copies + tables[:AHEAD]:
        copy.start()
    for copy in copies:
        copy.wait()
    for m in range(ORD):
        if m + AHEAD < ORD:
            tables[m + AHEAD].start()
        if m == ORD // 2:
            last.start()
        tables[m].wait()
        lat = modes[:, HALVES * m : HALVES * (m + 1), :].reshape(SHELLS * HALVES, NLAT)
        forcing = lax.dot_general(
            lat, table[m], (((1,), (1,)), ((), ())), preferred_element_type=F32
        )
        right_side = fields[:, m].reshape(SHELLS * HALVES, DEG) + forcing
        for tile in range(TILES):
            row = (m * TILES + tile) * HALVES
            solved[:, row : row + HALVES, :] = right_side[
                :, tile * LANES : (tile + 1) * LANES
            ].reshape(SHELLS, HALVES, LANES)
    last.wait()
    value = solved[0] * inverses[0]
    solved[0] = value
    for i in range(1, SHELLS):
        value = (solved[i] + shell[1, i] * value) * inverses[i]
        solved[i] = value
    ends[1] = value.astype(BF16)
    for i in reversed(range(SHELLS - 1)):
        value = solved[i] + (shell[2, i] * inverses[i]) * value
        solved[i] = value
    ends[0] = value.astype(BF16)


def forcing_solve(me, shell, slots, legendre, field, pivots):
    return pl.pallas_call(
        forcing_kernel,
        out_shape=(
            jax.ShapeDtypeStruct((SHELLS, ROWS, LANES), F32),
            jax.ShapeDtypeStruct((2, ROWS, LANES), BF16),
        ),
        in_specs=[whole(pltpu.SMEM)] * 2 + [whole(pl.ANY)] * (3 + NMODE),
        out_specs=(whole(), whole()),
        scratch_shapes=[
            pltpu.VMEM((SHELLS, PAIRS, NLAT), BF16),
            pltpu.VMEM((ORD, DEG, NLAT), BF16),
            pltpu.VMEM((SHELLS, ORD, HALVES, DEG), F32),
            pltpu.VMEM((SHELLS, ROWS, LANES), F32),
            pltpu.SemaphoreType.DMA((NMODE + 2,)),
            pltpu.SemaphoreType.DMA((ORD,)),
        ],
        compiler_params=params(58),
        cost_estimate=cost(2 * 64 * DEG * NLAT * ORD, 16_000_000),
        name="forcing_solve",
    )(me, shell, field, pivots, legendre, *slots)


def chain_values(links, values, first, last):
    alphas = [first]
    for k in range(CHAIN):
        first_value, last_value = values[k]
        alpha = last_value + links(k, 3) * first_value
        if alphas[-1] is not None:
            alpha = alpha + links(k, 4) * alphas[-1]
        alphas.append(alpha)
    firsts = [None] * CHAIN + [last]
    for k in reversed(range(CHAIN)):
        value = links(k, 0) * values[k][0]
        if alphas[k] is not None:
            value = value + links(k, 1) * alphas[k]
        if firsts[k + 1] is not None:
            value = value + links(k, 2) * firsts[k + 1]
        firsts[k] = value
    return alphas, firsts


def boundary_values(links, alphas, firsts, shape):
    zero = jnp.zeros(shape, F32)
    pairs = []
    for k in range(CHAIN):
        before = zero if alphas[k] is None else alphas[k] + links(k, 5) * firsts[k]
        behind = zero if firsts[k + 1] is None else firsts[k + 1]
        pairs.append((before, behind))
    return pairs


def slot_copies(position, slots, held, sems):
    return [
        pltpu.make_async_copy(slot, held.at[lax.rem(position + CHAIN - s, CHAIN)], sems.at[s])
        for s, slot in enumerate(slots)
    ]


def inner_kernel(place, links, a, b, c, d, out, held, coefficients, sems):
    copies = slot_copies(place[1], (a, b, c, d), held, sems)
    copies.append(pltpu.make_async_copy(links, coefficients, sems.at[CHAIN]))
    for copy in copies:
        copy.start()
    for copy in copies:
        copy.wait()
    values = [(held[k, 0].astype(F32), held[k, 1].astype(F32)) for k in range(CHAIN)]
    alphas, firsts = chain_values(lambda k, n: coefficients[k, n], values, None, None)
    out[0] = firsts[0].astype(BF16)
    out[1] = alphas[CHAIN].astype(BF16)


def inner_join(place, links, slots):
    return pl.pallas_call(
        inner_kernel,
        out_shape=jax.ShapeDtypeStruct((2, ROWS, LANES), BF16),
        in_specs=[whole(pltpu.SMEM)] + [whole(pl.ANY)] * 5,
        out_specs=whole(),
        scratch_shapes=[
            pltpu.VMEM((CHAIN, 2, ROWS, LANES), BF16),
            pltpu.VMEM((CHAIN, 6, ROWS, LANES), F32),
            pltpu.SemaphoreType.DMA((CHAIN + 1,)),
        ],
        compiler_params=params(12),
        cost_estimate=cost(1_000_000, 2_000_000),
        name="inner_join",
    )(place, links, *slots)


PIECES = 4
PIECE = SHELLS // PIECES


def final_kernel(place, inner, outer, a, b, c, d, e, f, g, h, solved, left, right, out, *scratch):
    near, far, near_links, far_links, pairs, terms, result, sems, term_sems, out_sems = scratch
    copies = slot_copies(place[0], (e, f, g, h), far, sems.at[0])
    copies.append(pltpu.make_async_copy(outer, far_links, sems.at[0, CHAIN]))
    copies += slot_copies(place[1], (a, b, c, d), near, sems.at[1])
    copies.append(pltpu.make_async_copy(inner, near_links, sems.at[1, CHAIN]))
    term_copies = [
        pltpu.make_async_copy(source, terms.at[n], term_sems.at[n])
        for n, source in enumerate((solved, left, right))
    ]
    for copy in copies + term_copies:
        copy.start()
    for copy in copies:
        copy.wait()
    first = last = None
    for level, (held, links) in enumerate(((far, far_links), (near, near_links))):
        values = [(held[k, 0].astype(F32), held[k, 1].astype(F32)) for k in range(CHAIN)]
        read = lambda k, n, links=links: links[k, n]
        alphas, firsts = chain_values(read, values, first, last)
        found = boundary_values(read, alphas, firsts, (ROWS, LANES))
        for k, (before, behind) in enumerate(found):
            pairs[k, 0] = before
            pairs[k, 1] = behind
        first, last = pairs[place[level], 0], pairs[place[level], 1]
    for copy in term_copies:
        copy.wait()
    sent = []
    for piece in range(PIECES):
        for i in range(piece * PIECE, (piece + 1) * PIECE):
            value = terms[0, i] + terms[1, i] * first + terms[2, i] * last
            value = value.reshape(ORD, TILES, HALVES, LANES)
            for tile in range(TILES):
                result[i, :, :, tile * LANES : (tile + 1) * LANES] = value[:, tile]
        here = pl.ds(piece * PIECE, PIECE)
        sent.append(pltpu.make_async_copy(result.at[here], out.at[here], out_sems.at[piece]))
        sent[-1].start()
    for copy in sent:
        copy.wait()


def final_join(place, inner, outer, slots, super_slots, solved, left, right):
    return pl.pallas_call(
        final_kernel,
        out_shape=jax.ShapeDtypeStruct((SHELLS, ORD, HALVES, DEG), F32),
        in_specs=[whole(pltpu.SMEM)] + [whole(pl.ANY)] * 13,
        out_specs=whole(pl.ANY),
        scratch_shapes=[
            pltpu.VMEM((CHAIN, 2, ROWS, LANES), BF16),
            pltpu.VMEM((CHAIN, 2, ROWS, LANES), BF16),
            pltpu.VMEM((CHAIN, 6, ROWS, LANES), F32),
            pltpu.VMEM((CHAIN, 6, ROWS, LANES), F32),
            pltpu.VMEM((CHAIN, 2, ROWS, LANES), F32),
            pltpu.VMEM((3, SHELLS, ROWS, LANES), F32),
            pltpu.VMEM((SHELLS, ORD, HALVES, DEG), F32),
            pltpu.SemaphoreType.DMA((2, CHAIN + 1)),
            pltpu.SemaphoreType.DMA((3,)),
            pltpu.SemaphoreType.DMA((PIECES,)),
        ],
        compiler_params=params(24),
        cost_estimate=cost(3_000_000, 9_000_000),
        name="final_join",
    )(place, inner, outer, *slots, *super_slots, solved, left, right)


def shifted(array, axis, step):
    size = lax.axis_size(axis)
    return lax.ppermute(array, axis, [(i, (i + step) % size) for i in range(size)])


def ring(array, axis):
    return [array] + [shifted(array, axis, step) for step in range(1, CHAIN)]


def on_device(scalar_field, radial_flow, legendre, diffusivity):
    synth, analysis = (jnp.asarray(table) for table in longitude_tables(ORD * NMODE))
    mode = lax.axis_index(MODE).astype(jnp.int32)
    me = mode.reshape(1)
    firsts = list(synthesis(0, me, scalar_field, radial_flow, legendre))
    later, firsts[0] = lax.optimization_barrier((me, firsts[0]))
    seconds = synthesis(1, later, scalar_field, radial_flow, legendre)
    firsts, seconds = moved_all(firsts, False), moved_all(seconds, False)
    diffusivity, mode, firsts[4] = lax.optimization_barrier((diffusivity, mode, firsts[4]))

    nr_total = SHELLS * CHAIN * CHAIN
    place = jnp.stack([lax.axis_index(RADIAL[0]), lax.axis_index(RADIAL[1])]).astype(jnp.int32)
    shell_ids = lax.axis_index(RADIAL) * SHELLS + jnp.arange(SHELLS, dtype=jnp.int32)
    radius = (nr_total * 7 // 13 + shell_ids).astype(F32)
    shell = jnp.stack(
        [
            diffusivity,
            jnp.where(shell_ids > 0, diffusivity, 0.0),
            jnp.where(shell_ids < nr_total - 1, diffusivity, 0.0),
            radius * radius,
        ]
    )
    row = np.arange(ROWS)[:, None]
    local_degree = row // (TILES * HALVES) + row // HALVES % TILES * LANES + np.arange(LANES)[None]
    degree = (local_degree + mode * ORD).astype(F32)
    angular = degree * (degree + 1.0)
    pivots, left, right = block_matrix(shell, angular)
    near = jnp.concatenate(ring(diffusivity.reshape(1, SHELLS), RADIAL[1]))
    blocks = jnp.concatenate(ring(near, RADIAL[0]))
    inner, outer = levels(jnp.concatenate([place, mode.reshape(1)]), blocks)

    modes = moved_all(grid_product(me, synth, analysis, firsts, seconds), True)
    pivots, inner, outer = lax.optimization_barrier((pivots, inner, outer))
    solved, own = forcing_solve(me, shell, modes, legendre, scalar_field, pivots)
    slots = ring(own, RADIAL[1])
    super_slots = ring(inner_join(place, inner, slots), RADIAL[0])
    return final_join(place, inner, outer, slots, super_slots, solved, left, right)


def solution(mesh):
    finer = Mesh(
        mesh.devices.reshape(4, 4, 4, 2), ("radial_0", "radial_1", "mode_0", "mode_1")
    )
    return jax.shard_map(
        on_device,
        mesh=finer,
        in_specs=(
            P(RADIAL, MODE, None, None),
            P(RADIAL, MODE, None, None),
            P(MODE, None, None),
            P(RADIAL),
        ),
        out_specs=P(RADIAL, MODE, None, None),
        check_vma=False,
    )
```

```python
import functools
import math

import jax
import jax.numpy as jnp
import ml_dtypes
import numpy as np
from jax import lax
from jax.experimental import pallas as pl
from jax.experimental.pallas import tpu as pltpu
from jax.sharding import Mesh
from jax.sharding import PartitionSpec as P

F32, BF16 = jnp.float32, jnp.bfloat16
MODE = ("mode_0", "mode_1")
RADIAL = ("radial_0", "radial_1")
NLON = 1536
POINTS = 384
LANES = 128
SHELLS, ORD, HALVES, DEG, NLAT = 32, 16, 2, 384, 768
TILES = DEG // LANES
ROWS = ORD * TILES * HALVES
NMODE = 8
NSHELL = SHELLS // NMODE
PAIRS = ORD * HALVES


def params(mebibytes=56):
    return pltpu.CompilerParams(vmem_limit_bytes=mebibytes * 2**20)


def cost(flops, nbytes):
    return pl.CostEstimate(flops=flops, bytes_accessed=nbytes, transcendentals=0)


def whole(space=pltpu.VMEM):
    return pl.BlockSpec(memory_space=space)


def fixed(shape):
    return pl.BlockSpec(shape, lambda *_: (0,) * len(shape))


def longitude_tables(orders):
    step = NLON // POINTS
    points = np.arange(POINTS) * step
    phase = (np.arange(orders)[:, None] * points[None, :]) % NLON
    angle = phase * (2.0 * math.pi / NLON)
    paired = np.stack([np.cos(angle), -np.sin(angle)], axis=1).reshape(2 * orders, POINTS)
    synth = (paired / math.sqrt(orders)).astype(np.float32).astype(ml_dtypes.bfloat16)
    analysis = (paired * math.sqrt(2.0 / NLON)).astype(np.float32).astype(ml_dtypes.bfloat16)
    return synth.T.copy(), (analysis.astype(np.float32) * step).astype(ml_dtypes.bfloat16)


def row_of(order, tile, half):
    return (order * TILES + tile) * HALVES + half


HALF = ORD // 2
PAIRS_HALF = HALF * HALVES
AHEAD = 4


def moved(device, k, back):
    z, core = device // 2, device % 2
    ahead = 1 - 2 * core
    steps, other = (
        (0, 0),
        (2, 0),
        (2, 1),
        (ahead, 0),
        (-ahead, 0),
        (ahead, 1),
        (-ahead, 1),
        (0, 1),
    )[k]
    if back and k in (3, 4):
        steps = -steps
    core = 1 - core if other else core
    return (z + steps + 4) % 4 * 2 + core


def moved_all(arrays, back):
    sent = [arrays[0]]
    for k in range(1, NMODE):
        pairs = [(d, moved(d, k, back)) for d in range(NMODE)]
        sent.append(lax.ppermute(arrays[k], MODE, pairs))
    return sent


def synthesis_kernel(half, me, field, flow, legendre, *refs):
    outs, (fields, flows, table, lat, sems, table_sems, out_sems) = refs[:NMODE], refs[NMODE:]
    orders = pl.ds(half * HALF, HALF)
    copies = [
        pltpu.make_async_copy(field.at[:, orders], fields, sems.at[0]),
        pltpu.make_async_copy(flow.at[:, orders], flows, sems.at[1]),
    ]
    tables = [
        pltpu.make_async_copy(legendre.at[half * HALF + m], table.at[m], table_sems.at[m])
        for m in range(HALF)
    ]
    for copy in copies + tables[:AHEAD]:
        copy.start()
    for copy in copies:
        copy.wait()
    for m in range(HALF):
        if m + AHEAD < HALF:
            tables[m + AHEAD].start()
        spectral = jnp.concatenate(
            [source[:, m].reshape(SHELLS * HALVES, DEG) for source in (fields, flows)], axis=0
        ).astype(BF16)
        tables[m].wait()
        values = jnp.dot(spectral, table[m], preferred_element_type=F32).astype(BF16)
        for f in range(2):
            mine = values[f * SHELLS * HALVES : (f + 1) * SHELLS * HALVES]
            lat[:, f, :, HALVES * m : HALVES * (m + 1), :] = mine.reshape(
                NMODE, NSHELL, HALVES, NLAT
            )
    sent = []
    for k in range(NMODE):
        source = lat.at[moved(me[0], k, False)]
        sent.append(pltpu.make_async_copy(source, outs[k], out_sems.at[k]))
        sent[-1].start()
    for copy in sent:
        copy.wait()


def synthesis(half, me, field, flow, legendre):
    shape = jax.ShapeDtypeStruct((2, NSHELL, PAIRS_HALF, NLAT), BF16)
    return pl.pallas_call(
        functools.partial(synthesis_kernel, half),
        out_shape=(shape,) * NMODE,
        in_specs=[whole(pltpu.SMEM)] + [whole(pl.ANY)] * 3,
        out_specs=(whole(pl.ANY),) * NMODE,
        scratch_shapes=[
            pltpu.VMEM((SHELLS, HALF, HALVES, DEG), F32),
            pltpu.VMEM((SHELLS, HALF, HALVES, DEG), F32),
            pltpu.VMEM((HALF, DEG, NLAT), BF16),
            pltpu.VMEM((NMODE, 2, NSHELL, PAIRS_HALF, NLAT), BF16),
            pltpu.SemaphoreType.DMA((2,)),
            pltpu.SemaphoreType.DMA((HALF,)),
            pltpu.SemaphoreType.DMA((NMODE,)),
        ],
        compiler_params=params(58),
        cost_estimate=cost(2 * 128 * DEG * NLAT * HALF, 8_000_000),
        name="synthesis",
    )(me, field, flow, legendre)


def grid_kernel(me, synth, analysis, *refs):
    firsts, seconds = refs[:NMODE], refs[NMODE : 2 * NMODE]
    outs = refs[2 * NMODE : 3 * NMODE]
    lat, modes, sems, out_sems = refs[3 * NMODE :]
    arrived = []
    for k in range(NMODE):
        top = moved(me[0], k, True) * PAIRS
        for h, source in enumerate((firsts[k], seconds[k])):
            place = lat.at[:, :, pl.ds(pl.multiple_of(top + h * PAIRS_HALF, PAIRS_HALF), PAIRS_HALF)]
            arrived.append(pltpu.make_async_copy(source, place, sems.at[k, h]))
            arrived[-1].start()
    for copy in arrived:
        copy.wait()
    sent = []
    for r in range(NSHELL):
        field = jnp.dot(synth[...], lat[0, r], preferred_element_type=F32)
        flow = jnp.dot(synth[...], lat[1, r], preferred_element_type=F32)
        product = (field * flow).astype(BF16)
        found = jnp.dot(analysis[...], product, preferred_element_type=F32).astype(BF16)
        modes[:, r] = found.reshape(NMODE, PAIRS, NLAT)
        for k in range(NMODE):
            source = modes.at[moved(me[0], k, True), r]
            sent.append(pltpu.make_async_copy(source, outs[k].at[r], out_sems.at[r, k]))
            sent[-1].start()
    for copy in sent:
        copy.wait()


def grid_product(me, synth, analysis, firsts, seconds):
    shape = jax.ShapeDtypeStruct((NSHELL, PAIRS, NLAT), BF16)
    return pl.pallas_call(
        grid_kernel,
        out_shape=(shape,) * NMODE,
        in_specs=[whole(pltpu.SMEM), whole(), whole()] + [whole(pl.ANY)] * (2 * NMODE),
        out_specs=(whole(pl.ANY),) * NMODE,
        scratch_shapes=[
            pltpu.VMEM((2, NSHELL, NMODE * PAIRS, NLAT), BF16),
            pltpu.VMEM((NMODE, NSHELL, PAIRS, NLAT), BF16),
            pltpu.SemaphoreType.DMA((NMODE, 2)),
            pltpu.SemaphoreType.DMA((NSHELL, NMODE)),
        ],
        compiler_params=params(58),
        cost_estimate=cost(3 * 2 * POINTS * 256 * NLAT * NSHELL, 5_000_000),
        name="grid_product",
    )(me, synth, analysis, *firsts, *seconds)


def block_matrix_kernel(shell, angular, pivots, left, right):
    ang = angular[...]
    ratio = jnp.zeros((ROWS, LANES), F32)
    answer = jnp.ones((ROWS, LANES), F32)
    ratios = []
    for i in range(SHELLS):
        kappa, low, up, radius2 = shell[0, i], shell[1, i], shell[2, i], shell[3, i]
        diagonal = 1.0 + 2.0 * kappa + kappa * ang / radius2
        inverse = 1.0 / (diagonal - low * ratio)
        ratio = up * inverse
        answer = low * inverse * answer
        pivots[i] = inverse
        left[i] = answer
    before = left[SHELLS - 1]
    behind = ratio
    right[SHELLS - 1] = behind
    for i in reversed(range(SHELLS - 1)):
        ratio = shell[2, i] * pivots[i]
        before = left[i] + ratio * before
        behind = ratio * behind
        left[i] = before
        right[i] = behind


def block_matrix(shell, angular):
    big = jax.ShapeDtypeStruct((SHELLS, ROWS, LANES), F32)
    return pl.pallas_call(
        block_matrix_kernel,
        out_shape=(big, big, big),
        in_specs=[whole(pltpu.SMEM), whole()],
        out_specs=(whole(),) * 3,
        compiler_params=params(16),
        cost_estimate=cost(10_000_000, 6_000_000),
        name="block_matrix",
    )(shell, angular)


CHAIN = 4


def chain_matrix(blocks):
    links = []
    beta = None
    for first_left, first_right, last_left, last_right in blocks:
        if beta is None:
            den = jnp.ones_like(first_left)
            beta = jnp.zeros_like(first_left)
        else:
            den = 1.0 / (1.0 - first_left * beta)
        extra = last_left * beta * den
        links.append(
            (den, den * first_left, den * first_right, extra, last_left * den, beta)
        )
        beta = last_right + extra * first_right
    alpha = None
    alphas = []
    for link in links:
        alphas.append(alpha)
        alpha = link[4] if alpha is None else link[4] * alpha
    before = None
    behind = None
    for link, start in zip(reversed(links), reversed(alphas)):
        own = link[1] if start is None else link[1] * start
        before = own if before is None else own + link[2] * before
        behind = link[2] if behind is None else link[2] * behind
    return links, (before, behind, alpha, beta)


DEGREES = 512
LINKS = 6


def level_kernel(where, a, b, c, d, inner, outer, slots, ordered, factors, links_held, table):
    x, y, mode = where[0], where[1], where[2]
    for n, source in enumerate((a, b, c, d)):
        slots[n * CHAIN : (n + 1) * CHAIN, :] = source[...]
    for k in range(CHAIN):
        for first in range(8):
            slot = lax.rem(x + CHAIN - first % CHAIN, CHAIN) * CHAIN + lax.rem(y + CHAIN - k, CHAIN)
            ordered[k, first : first + 1, :] = slots[pl.ds(slot, 1), :]
    degree = lax.broadcasted_iota(jnp.int32, (1, 1, DEGREES), 2).astype(F32)
    angular = degree * (degree + 1.0)
    shape = (CHAIN, 8, 1)
    block = lax.broadcasted_iota(jnp.int32, shape, 1) % CHAIN * CHAIN
    block = block + lax.broadcasted_iota(jnp.int32, shape, 0)
    total = CHAIN * CHAIN * SHELLS

    def kappas(i):
        kappa = ordered[:, :, i : i + 1]
        low, up = kappa, kappa
        if i == 0:
            low = jnp.where(block == 0, 0.0, kappa)
        if i == SHELLS - 1:
            up = jnp.where(block == CHAIN * CHAIN - 1, 0.0, kappa)
        return kappa, low, up

    ratio = jnp.zeros((CHAIN, 8, DEGREES), F32)
    answer = jnp.ones((CHAIN, 8, DEGREES), F32)
    for i in range(SHELLS):
        kappa, low, up = kappas(i)
        radius = (total * 7 // 13 + block * SHELLS + i).astype(F32)
        diagonal = 1.0 + 2.0 * kappa + kappa * angular / (radius * radius)
        inverse = 1.0 / (diagonal - low * ratio)
        ratio = up * inverse
        answer = low * inverse * answer
        factors[0, i] = ratio
        factors[1, i] = answer
    before, behind = answer, ratio
    last_left, last_right = before, behind
    for i in reversed(range(SHELLS - 1)):
        before = factors[1, i] + factors[0, i] * before
        behind = factors[0, i] * behind
    ends = (before, behind, last_left, last_right)
    links, supers = chain_matrix([tuple(end[k] for end in ends) for k in range(CHAIN)])
    for k in range(CHAIN):
        for n in range(LINKS):
            links_held[k * LINKS + n] = links[k][n]
    far, _ = chain_matrix([tuple(end[k : k + 1] for end in supers) for k in range(CHAIN)])
    for k in range(CHAIN):
        for n in range(LINKS):
            row = k * LINKS + n
            table[row : row + 1, :] = links_held[row, pl.ds(x, 1), :]
            row_far = CHAIN * LINKS + row
            table[row_far : row_far + 1, :] = far[k][n]
    values = table[...]
    count = CHAIN * LINKS
    for m in range(ORD):
        here = pltpu.roll(values, DEGREES - (mode * ORD + m), 1)
        for tile in range(TILES):
            found = here[:, tile * LANES : (tile + 1) * LANES]
            for half in range(HALVES):
                rows = pl.ds(row_of(m, tile, half), count, stride=ROWS)
                inner[rows, :] = found[:count]
                outer[rows, :] = found[count:]


def levels(where, blocks):
    count = CHAIN * LINKS
    shape = jax.ShapeDtypeStruct((count * ROWS, LANES), F32)
    outs = pl.pallas_call(
        level_kernel,
        out_shape=(shape, shape),
        in_specs=[whole(pltpu.SMEM)] + [whole()] * CHAIN,
        out_specs=(whole(), whole()),
        scratch_shapes=[
            pltpu.VMEM((CHAIN * CHAIN, SHELLS), F32),
            pltpu.VMEM((CHAIN, 8, SHELLS), F32),
            pltpu.VMEM((2, SHELLS, CHAIN, 8, DEGREES), F32),
            pltpu.VMEM((count, 8, DEGREES), F32),
            pltpu.VMEM((2 * count, DEGREES), F32),
        ],
        compiler_params=params(20),
        cost_estimate=cost(10_000_000, 8_000_000),
        name="levels",
    )(where, *blocks)
    return [out.reshape(CHAIN, LINKS, ROWS, LANES) for out in outs]


def forcing_kernel(me, shell, field, pivots, legendre, *refs):
    slots = refs[:NMODE]
    solved, ends, modes, table, sems, table_sems = refs[NMODE:]
    copies = [
        pltpu.make_async_copy(
            slots[k], modes.at[pl.ds(moved(me[0], k, False) * NSHELL, NSHELL)], sems.at[k]
        )
        for k in range(NMODE)
    ]
    tables = [
        pltpu.make_async_copy(legendre.at[m], table.at[m], table_sems.at[m]) for m in range(ORD)
    ]
    for copy in copies + tables[:AHEAD]:
        copy.start()
    for copy in copies:
        copy.wait()
    for m in range(ORD):
        if m + AHEAD < ORD:
            tables[m + AHEAD].start()
        tables[m].wait()
        lat = modes[:, HALVES * m : HALVES * (m + 1), :].reshape(SHELLS * HALVES, NLAT)
        forcing = lax.dot_general(
            lat, table[m], (((1,), (1,)), ((), ())), preferred_element_type=F32
        )
        right_side = field[:, m].reshape(SHELLS * HALVES, DEG) + forcing
        for tile in range(TILES):
            row = (m * TILES + tile) * HALVES
            solved[:, row : row + HALVES, :] = right_side[
                :, tile * LANES : (tile + 1) * LANES
            ].reshape(SHELLS, HALVES, LANES)
    value = solved[0] * pivots[0]
    solved[0] = value
    for i in range(1, SHELLS):
        value = (solved[i] + shell[1, i] * value) * pivots[i]
        solved[i] = value
    ends[1] = value.astype(BF16)
    for i in reversed(range(SHELLS - 1)):
        value = solved[i] + (shell[2, i] * pivots[i]) * value
        solved[i] = value
    ends[0] = value.astype(BF16)


def forcing_solve(me, shell, slots, legendre, field, pivots):
    return pl.pallas_call(
        forcing_kernel,
        out_shape=(
            jax.ShapeDtypeStruct((SHELLS, ROWS, LANES), F32),
            jax.ShapeDtypeStruct((2, ROWS, LANES), BF16),
        ),
        in_specs=[whole(pltpu.SMEM)] * 2 + [whole()] * 2 + [whole(pl.ANY)] * (1 + NMODE),
        out_specs=(whole(), whole()),
        scratch_shapes=[
            pltpu.VMEM((SHELLS, PAIRS, NLAT), BF16),
            pltpu.VMEM((ORD, DEG, NLAT), BF16),
            pltpu.SemaphoreType.DMA((NMODE,)),
            pltpu.SemaphoreType.DMA((ORD,)),
        ],
        compiler_params=params(50),
        cost_estimate=cost(2 * 64 * DEG * NLAT * ORD, 16_000_000),
        name="forcing_solve",
    )(me, shell, field, pivots, legendre, *slots)


def chain_values(links, values, first, last):
    alphas = [first]
    for k in range(CHAIN):
        first_value, last_value = values[k]
        alpha = last_value + links(k, 3) * first_value
        if alphas[-1] is not None:
            alpha = alpha + links(k, 4) * alphas[-1]
        alphas.append(alpha)
    firsts = [None] * CHAIN + [last]
    for k in reversed(range(CHAIN)):
        value = links(k, 0) * values[k][0]
        if alphas[k] is not None:
            value = value + links(k, 1) * alphas[k]
        if firsts[k + 1] is not None:
            value = value + links(k, 2) * firsts[k + 1]
        firsts[k] = value
    return alphas, firsts


def boundary_values(links, alphas, firsts, shape):
    zero = jnp.zeros(shape, F32)
    pairs = []
    for k in range(CHAIN):
        before = zero if alphas[k] is None else alphas[k] + links(k, 5) * firsts[k]
        behind = zero if firsts[k + 1] is None else firsts[k + 1]
        pairs.append((before, behind))
    return pairs


def slot_copies(position, slots, held, sems):
    return [
        pltpu.make_async_copy(slot, held.at[lax.rem(position + CHAIN - s, CHAIN)], sems.at[s])
        for s, slot in enumerate(slots)
    ]


def inner_kernel(place, links, a, b, c, d, out, held, coefficients, sems):
    copies = slot_copies(place[1], (a, b, c, d), held, sems)
    copies.append(pltpu.make_async_copy(links, coefficients, sems.at[CHAIN]))
    for copy in copies:
        copy.start()
    for copy in copies:
        copy.wait()
    values = [(held[k, 0].astype(F32), held[k, 1].astype(F32)) for k in range(CHAIN)]
    alphas, firsts = chain_values(lambda k, n: coefficients[k, n], values, None, None)
    out[0] = firsts[0].astype(BF16)
    out[1] = alphas[CHAIN].astype(BF16)


def inner_join(place, links, slots):
    return pl.pallas_call(
        inner_kernel,
        out_shape=jax.ShapeDtypeStruct((2, ROWS, LANES), BF16),
        in_specs=[whole(pltpu.SMEM)] + [whole(pl.ANY)] * 5,
        out_specs=whole(),
        scratch_shapes=[
            pltpu.VMEM((CHAIN, 2, ROWS, LANES), BF16),
            pltpu.VMEM((CHAIN, 6, ROWS, LANES), F32),
            pltpu.SemaphoreType.DMA((CHAIN + 1,)),
        ],
        compiler_params=params(12),
        cost_estimate=cost(1_000_000, 2_000_000),
        name="inner_join",
    )(place, links, *slots)


PIECES = 4
PIECE = SHELLS // PIECES


def final_kernel(place, inner, outer, a, b, c, d, e, f, g, h, solved, left, right, out, *scratch):
    near, far, near_links, far_links, pairs, terms, result, sems, term_sems, out_sems = scratch
    copies = slot_copies(place[0], (e, f, g, h), far, sems.at[0])
    copies.append(pltpu.make_async_copy(outer, far_links, sems.at[0, CHAIN]))
    copies += slot_copies(place[1], (a, b, c, d), near, sems.at[1])
    copies.append(pltpu.make_async_copy(inner, near_links, sems.at[1, CHAIN]))
    term_copies = [
        pltpu.make_async_copy(source, terms.at[n], term_sems.at[n])
        for n, source in enumerate((solved, left, right))
    ]
    for copy in copies + term_copies:
        copy.start()
    for copy in copies:
        copy.wait()
    first = last = None
    for level, (held, links) in enumerate(((far, far_links), (near, near_links))):
        values = [(held[k, 0].astype(F32), held[k, 1].astype(F32)) for k in range(CHAIN)]
        read = lambda k, n, links=links: links[k, n]
        alphas, firsts = chain_values(read, values, first, last)
        found = boundary_values(read, alphas, firsts, (ROWS, LANES))
        for k, (before, behind) in enumerate(found):
            pairs[k, 0] = before
            pairs[k, 1] = behind
        first, last = pairs[place[level], 0], pairs[place[level], 1]
    for copy in term_copies:
        copy.wait()
    sent = []
    for piece in range(PIECES):
        for i in range(piece * PIECE, (piece + 1) * PIECE):
            value = terms[0, i] + terms[1, i] * first + terms[2, i] * last
            value = value.reshape(ORD, TILES, HALVES, LANES)
            for tile in range(TILES):
                result[i, :, :, tile * LANES : (tile + 1) * LANES] = value[:, tile]
        here = pl.ds(piece * PIECE, PIECE)
        sent.append(pltpu.make_async_copy(result.at[here], out.at[here], out_sems.at[piece]))
        sent[-1].start()
    for copy in sent:
        copy.wait()


def final_join(place, inner, outer, slots, super_slots, solved, left, right):
    return pl.pallas_call(
        final_kernel,
        out_shape=jax.ShapeDtypeStruct((SHELLS, ORD, HALVES, DEG), F32),
        in_specs=[whole(pltpu.SMEM)] + [whole(pl.ANY)] * 13,
        out_specs=whole(pl.ANY),
        scratch_shapes=[
            pltpu.VMEM((CHAIN, 2, ROWS, LANES), BF16),
            pltpu.VMEM((CHAIN, 2, ROWS, LANES), BF16),
            pltpu.VMEM((CHAIN, 6, ROWS, LANES), F32),
            pltpu.VMEM((CHAIN, 6, ROWS, LANES), F32),
            pltpu.VMEM((CHAIN, 2, ROWS, LANES), F32),
            pltpu.VMEM((3, SHELLS, ROWS, LANES), F32),
            pltpu.VMEM((SHELLS, ORD, HALVES, DEG), F32),
            pltpu.SemaphoreType.DMA((2, CHAIN + 1)),
            pltpu.SemaphoreType.DMA((3,)),
            pltpu.SemaphoreType.DMA((PIECES,)),
        ],
        compiler_params=params(24),
        cost_estimate=cost(3_000_000, 9_000_000),
        name="final_join",
    )(place, inner, outer, *slots, *super_slots, solved, left, right)


def shifted(array, axis, step):
    size = lax.axis_size(axis)
    return lax.ppermute(array, axis, [(i, (i + step) % size) for i in range(size)])


def ring(array, axis):
    return [array] + [shifted(array, axis, step) for step in range(1, CHAIN)]


def on_device(scalar_field, radial_flow, legendre, diffusivity):
    synth, analysis = (jnp.asarray(table) for table in longitude_tables(ORD * NMODE))
    mode = lax.axis_index(MODE).astype(jnp.int32)
    me = mode.reshape(1)
    firsts = list(synthesis(0, me, scalar_field, radial_flow, legendre))
    later, firsts[0] = lax.optimization_barrier((me, firsts[0]))
    seconds = synthesis(1, later, scalar_field, radial_flow, legendre)
    firsts, seconds = moved_all(firsts, False), moved_all(seconds, False)
    diffusivity, mode, firsts[4] = lax.optimization_barrier((diffusivity, mode, firsts[4]))

    nr_total = SHELLS * CHAIN * CHAIN
    place = jnp.stack([lax.axis_index(RADIAL[0]), lax.axis_index(RADIAL[1])]).astype(jnp.int32)
    shell_ids = lax.axis_index(RADIAL) * SHELLS + jnp.arange(SHELLS, dtype=jnp.int32)
    radius = (nr_total * 7 // 13 + shell_ids).astype(F32)
    shell = jnp.stack(
        [
            diffusivity,
            jnp.where(shell_ids > 0, diffusivity, 0.0),
            jnp.where(shell_ids < nr_total - 1, diffusivity, 0.0),
            radius * radius,
        ]
    )
    row = np.arange(ROWS)[:, None]
    local_degree = row // (TILES * HALVES) + row // HALVES % TILES * LANES + np.arange(LANES)[None]
    degree = (local_degree + mode * ORD).astype(F32)
    angular = degree * (degree + 1.0)
    pivots, left, right = block_matrix(shell, angular)
    near = jnp.concatenate(ring(diffusivity.reshape(1, SHELLS), RADIAL[1]))
    blocks = ring(near, RADIAL[0])
    inner, outer = levels(jnp.concatenate([place, mode.reshape(1)]), blocks)

    modes = moved_all(grid_product(me, synth, analysis, firsts, seconds), True)
    pivots, inner, outer = lax.optimization_barrier((pivots, inner, outer))
    solved, own = forcing_solve(me, shell, modes, legendre, scalar_field, pivots)
    slots = ring(own, RADIAL[1])
    super_slots = ring(inner_join(place, inner, slots), RADIAL[0])
    return final_join(place, inner, outer, slots, super_slots, solved, left, right)


def solution(mesh):
    finer = Mesh(
        mesh.devices.reshape(4, 4, 4, 2), ("radial_0", "radial_1", "mode_0", "mode_1")
    )
    return jax.shard_map(
        on_device,
        mesh=finer,
        in_specs=(
            P(RADIAL, MODE, None, None),
            P(RADIAL, MODE, None, None),
            P(MODE, None, None),
            P(RADIAL),
        ),
        out_specs=P(RADIAL, MODE, None, None),
        check_vma=False,
    )
```

```python
import functools
import math

import jax
import jax.numpy as jnp
import ml_dtypes
import numpy as np
from jax import lax
from jax.experimental import pallas as pl
from jax.experimental.pallas import tpu as pltpu
from jax.sharding import Mesh
from jax.sharding import PartitionSpec as P

F32, BF16 = jnp.float32, jnp.bfloat16
MODE = ("mode_0", "mode_1")
RADIAL = ("radial_0", "radial_1")
NLON = 1536
POINTS = 384
LANES = 128
SHELLS, ORD, HALVES, DEG, NLAT = 32, 16, 2, 384, 768
TILES = DEG // LANES
ROWS = ORD * TILES * HALVES
NMODE = 8
NSHELL = SHELLS // NMODE
PAIRS = ORD * HALVES


def params(mebibytes=56):
    return pltpu.CompilerParams(vmem_limit_bytes=mebibytes * 2**20)


def cost(flops, nbytes):
    return pl.CostEstimate(flops=flops, bytes_accessed=nbytes, transcendentals=0)


def whole(space=pltpu.VMEM):
    return pl.BlockSpec(memory_space=space)


def fixed(shape):
    return pl.BlockSpec(shape, lambda *_: (0,) * len(shape))


def longitude_tables(orders):
    step = NLON // POINTS
    points = np.arange(POINTS) * step
    phase = (np.arange(orders)[:, None] * points[None, :]) % NLON
    angle = phase * (2.0 * math.pi / NLON)
    paired = np.stack([np.cos(angle), -np.sin(angle)], axis=1).reshape(2 * orders, POINTS)
    synth = (paired / math.sqrt(orders)).astype(np.float32).astype(ml_dtypes.bfloat16)
    analysis = (paired * math.sqrt(2.0 / NLON)).astype(np.float32).astype(ml_dtypes.bfloat16)
    return synth.T.copy(), (analysis.astype(np.float32) * step).astype(ml_dtypes.bfloat16)


def row_of(order, tile, half):
    return (order * TILES + tile) * HALVES + half


HALF = ORD // 2
PAIRS_HALF = HALF * HALVES
AHEAD = 4


def moved(device, k, back):
    z, core = device // 2, device % 2
    ahead = 1 - 2 * core
    steps, other = (
        (0, 0),
        (2, 0),
        (2, 1),
        (ahead, 0),
        (-ahead, 0),
        (ahead, 1),
        (-ahead, 1),
        (0, 1),
    )[k]
    if back and k in (3, 4):
        steps = -steps
    core = 1 - core if other else core
    return (z + steps + 4) % 4 * 2 + core


def moved_all(arrays, back):
    sent = [arrays[0]]
    for k in range(1, NMODE):
        pairs = [(d, moved(d, k, back)) for d in range(NMODE)]
        sent.append(lax.ppermute(arrays[k], MODE, pairs))
    return sent


def synthesis_kernel(half, me, field, flow, legendre, *refs):
    outs, (fields, flows, table, lat, sems, table_sems, out_sems) = refs[:NMODE], refs[NMODE:]
    orders = pl.ds(half * HALF, HALF)
    copies = [
        pltpu.make_async_copy(field.at[:, orders], fields, sems.at[0]),
        pltpu.make_async_copy(flow.at[:, orders], flows, sems.at[1]),
    ]
    tables = [
        pltpu.make_async_copy(legendre.at[half * HALF + m], table.at[m], table_sems.at[m])
        for m in range(HALF)
    ]
    for copy in copies + tables[:AHEAD]:
        copy.start()
    for copy in copies:
        copy.wait()
    for m in range(HALF):
        if m + AHEAD < HALF:
            tables[m + AHEAD].start()
        spectral = jnp.concatenate(
            [source[:, m].reshape(SHELLS * HALVES, DEG) for source in (fields, flows)], axis=0
        ).astype(BF16)
        tables[m].wait()
        values = jnp.dot(spectral, table[m], preferred_element_type=F32).astype(BF16)
        for f in range(2):
            mine = values[f * SHELLS * HALVES : (f + 1) * SHELLS * HALVES]
            lat[:, f, :, HALVES * m : HALVES * (m + 1), :] = mine.reshape(
                NMODE, NSHELL, HALVES, NLAT
            )
    sent = []
    for k in range(NMODE):
        source = lat.at[moved(me[0], k, False)]
        sent.append(pltpu.make_async_copy(source, outs[k], out_sems.at[k]))
        sent[-1].start()
    for copy in sent:
        copy.wait()


def synthesis(half, me, field, flow, legendre):
    shape = jax.ShapeDtypeStruct((2, NSHELL, PAIRS_HALF, NLAT), BF16)
    return pl.pallas_call(
        functools.partial(synthesis_kernel, half),
        out_shape=(shape,) * NMODE,
        in_specs=[whole(pltpu.SMEM)] + [whole(pl.ANY)] * 3,
        out_specs=(whole(pl.ANY),) * NMODE,
        scratch_shapes=[
            pltpu.VMEM((SHELLS, HALF, HALVES, DEG), F32),
            pltpu.VMEM((SHELLS, HALF, HALVES, DEG), F32),
            pltpu.VMEM((HALF, DEG, NLAT), BF16),
            pltpu.VMEM((NMODE, 2, NSHELL, PAIRS_HALF, NLAT), BF16),
            pltpu.SemaphoreType.DMA((2,)),
            pltpu.SemaphoreType.DMA((HALF,)),
            pltpu.SemaphoreType.DMA((NMODE,)),
        ],
        compiler_params=params(58),
        cost_estimate=cost(2 * 128 * DEG * NLAT * HALF, 8_000_000),
        name="synthesis",
    )(me, field, flow, legendre)


def grid_kernel(me, synth, analysis, *refs):
    firsts, seconds = refs[:NMODE], refs[NMODE : 2 * NMODE]
    outs = refs[2 * NMODE : 3 * NMODE]
    lat, modes, sems, out_sems = refs[3 * NMODE :]
    arrived = []
    for k in range(NMODE):
        top = moved(me[0], k, True) * PAIRS
        for h, source in enumerate((firsts[k], seconds[k])):
            place = lat.at[:, :, pl.ds(pl.multiple_of(top + h * PAIRS_HALF, PAIRS_HALF), PAIRS_HALF)]
            arrived.append(pltpu.make_async_copy(source, place, sems.at[k, h]))
            arrived[-1].start()
    for copy in arrived:
        copy.wait()
    sent = []
    for r in range(NSHELL):
        field = jnp.dot(synth[...], lat[0, r], preferred_element_type=F32)
        flow = jnp.dot(synth[...], lat[1, r], preferred_element_type=F32)
        product = (field * flow).astype(BF16)
        found = jnp.dot(analysis[...], product, preferred_element_type=F32).astype(BF16)
        modes[:, r] = found.reshape(NMODE, PAIRS, NLAT)
        for k in range(NMODE):
            source = modes.at[moved(me[0], k, True), r]
            sent.append(pltpu.make_async_copy(source, outs[k].at[r], out_sems.at[r, k]))
            sent[-1].start()
    for copy in sent:
        copy.wait()


def grid_product(me, synth, analysis, firsts, seconds):
    shape = jax.ShapeDtypeStruct((NSHELL, PAIRS, NLAT), BF16)
    return pl.pallas_call(
        grid_kernel,
        out_shape=(shape,) * NMODE,
        in_specs=[whole(pltpu.SMEM), whole(), whole()] + [whole(pl.ANY)] * (2 * NMODE),
        out_specs=(whole(pl.ANY),) * NMODE,
        scratch_shapes=[
            pltpu.VMEM((2, NSHELL, NMODE * PAIRS, NLAT), BF16),
            pltpu.VMEM((NMODE, NSHELL, PAIRS, NLAT), BF16),
            pltpu.SemaphoreType.DMA((NMODE, 2)),
            pltpu.SemaphoreType.DMA((NSHELL, NMODE)),
        ],
        compiler_params=params(58),
        cost_estimate=cost(3 * 2 * POINTS * 256 * NLAT * NSHELL, 5_000_000),
        name="grid_product",
    )(me, synth, analysis, *firsts, *seconds)


def block_matrix_kernel(shell, angular, pivots, left, right):
    ang = angular[...]
    ratio = jnp.zeros((ROWS, LANES), F32)
    answer = jnp.ones((ROWS, LANES), F32)
    ratios = []
    for i in range(SHELLS):
        kappa, low, up, radius2 = shell[0, i], shell[1, i], shell[2, i], shell[3, i]
        diagonal = 1.0 + 2.0 * kappa + kappa * ang / radius2
        inverse = 1.0 / (diagonal - low * ratio)
        ratio = up * inverse
        answer = low * inverse * answer
        pivots[i] = inverse
        left[i] = answer
    before = left[SHELLS - 1]
    behind = ratio
    right[SHELLS - 1] = behind
    for i in reversed(range(SHELLS - 1)):
        ratio = shell[2, i] * pivots[i]
        before = left[i] + ratio * before
        behind = ratio * behind
        left[i] = before
        right[i] = behind


def block_matrix(shell, angular):
    big = jax.ShapeDtypeStruct((SHELLS, ROWS, LANES), F32)
    return pl.pallas_call(
        block_matrix_kernel,
        out_shape=(big, big, big),
        in_specs=[whole(pltpu.SMEM), whole()],
        out_specs=(whole(),) * 3,
        compiler_params=params(16),
        cost_estimate=cost(10_000_000, 6_000_000),
        name="block_matrix",
    )(shell, angular)


CHAIN = 4


def chain_matrix(blocks):
    links = []
    beta = None
    for first_left, first_right, last_left, last_right in blocks:
        if beta is None:
            den = jnp.ones_like(first_left)
            beta = jnp.zeros_like(first_left)
        else:
            den = 1.0 / (1.0 - first_left * beta)
        extra = last_left * beta * den
        links.append(
            (den, den * first_left, den * first_right, extra, last_left * den, beta)
        )
        beta = last_right + extra * first_right
    alpha = None
    alphas = []
    for link in links:
        alphas.append(alpha)
        alpha = link[4] if alpha is None else link[4] * alpha
    before = None
    behind = None
    for link, start in zip(reversed(links), reversed(alphas)):
        own = link[1] if start is None else link[1] * start
        before = own if before is None else own + link[2] * before
        behind = link[2] if behind is None else link[2] * behind
    return links, (before, behind, alpha, beta)


DEGREES = 512
LINKS = 6


def level_kernel(where, a, b, c, d, inner, outer, slots, ordered, factors, links_held, table):
    x, y, mode = where[0], where[1], where[2]
    for n, source in enumerate((a, b, c, d)):
        slots[n * CHAIN : (n + 1) * CHAIN, :] = source[...]
    for k in range(CHAIN):
        for first in range(8):
            slot = lax.rem(x + CHAIN - first % CHAIN, CHAIN) * CHAIN + lax.rem(y + CHAIN - k, CHAIN)
            ordered[k, first : first + 1, :] = slots[pl.ds(slot, 1), :]
    degree = lax.broadcasted_iota(jnp.int32, (1, 1, DEGREES), 2).astype(F32)
    angular = degree * (degree + 1.0)
    shape = (CHAIN, 8, 1)
    block = lax.broadcasted_iota(jnp.int32, shape, 1) % CHAIN * CHAIN
    block = block + lax.broadcasted_iota(jnp.int32, shape, 0)
    total = CHAIN * CHAIN * SHELLS

    def kappas(i):
        kappa = ordered[:, :, i : i + 1]
        low, up = kappa, kappa
        if i == 0:
            low = jnp.where(block == 0, 0.0, kappa)
        if i == SHELLS - 1:
            up = jnp.where(block == CHAIN * CHAIN - 1, 0.0, kappa)
        return kappa, low, up

    ratio = jnp.zeros((CHAIN, 8, DEGREES), F32)
    answer = jnp.ones((CHAIN, 8, DEGREES), F32)
    for i in range(SHELLS):
        kappa, low, up = kappas(i)
        radius = (total * 7 // 13 + block * SHELLS + i).astype(F32)
        diagonal = 1.0 + 2.0 * kappa + kappa * angular / (radius * radius)
        inverse = 1.0 / (diagonal - low * ratio)
        ratio = up * inverse
        answer = low * inverse * answer
        factors[0, i] = ratio
        factors[1, i] = answer
    before, behind = answer, ratio
    last_left, last_right = before, behind
    for i in reversed(range(SHELLS - 1)):
        before = factors[1, i] + factors[0, i] * before
        behind = factors[0, i] * behind
    ends = (before, behind, last_left, last_right)
    links, supers = chain_matrix([tuple(end[k] for end in ends) for k in range(CHAIN)])
    for k in range(CHAIN):
        for n in range(LINKS):
            links_held[k * LINKS + n] = links[k][n]
    far, _ = chain_matrix([tuple(end[k : k + 1] for end in supers) for k in range(CHAIN)])
    for k in range(CHAIN):
        for n in range(LINKS):
            row = k * LINKS + n
            table[row : row + 1, :] = links_held[row, pl.ds(x, 1), :]
            row_far = CHAIN * LINKS + row
            table[row_far : row_far + 1, :] = far[k][n]
    values = table[...]
    count = CHAIN * LINKS
    for m in range(ORD):
        here = pltpu.roll(values, DEGREES - (mode * ORD + m), 1)
        for tile in range(TILES):
            found = here[:, tile * LANES : (tile + 1) * LANES]
            for half in range(HALVES):
                rows = pl.ds(row_of(m, tile, half), count, stride=ROWS)
                inner[rows, :] = found[:count]
                outer[rows, :] = found[count:]


def levels(where, blocks):
    count = CHAIN * LINKS
    shape = jax.ShapeDtypeStruct((count * ROWS, LANES), F32)
    outs = pl.pallas_call(
        level_kernel,
        out_shape=(shape, shape),
        in_specs=[whole(pltpu.SMEM)] + [whole()] * CHAIN,
        out_specs=(whole(), whole()),
        scratch_shapes=[
            pltpu.VMEM((CHAIN * CHAIN, SHELLS), F32),
            pltpu.VMEM((CHAIN, 8, SHELLS), F32),
            pltpu.VMEM((2, SHELLS, CHAIN, 8, DEGREES), F32),
            pltpu.VMEM((count, 8, DEGREES), F32),
            pltpu.VMEM((2 * count, DEGREES), F32),
        ],
        compiler_params=params(20),
        cost_estimate=cost(10_000_000, 8_000_000),
        name="levels",
    )(where, *blocks)
    return [out.reshape(CHAIN, LINKS, ROWS, LANES) for out in outs]


def forcing_kernel(me, shell, field, pivots, legendre, *refs):
    slots = refs[:NMODE]
    solved, ends, modes, sems = refs[NMODE:]
    copies = [
        pltpu.make_async_copy(
            slots[k], modes.at[pl.ds(moved(me[0], k, False) * NSHELL, NSHELL)], sems.at[k]
        )
        for k in range(NMODE)
    ]
    for copy in copies:
        copy.start()
    for copy in copies:
        copy.wait()
    for m in range(ORD):
        lat = modes[:, HALVES * m : HALVES * (m + 1), :].reshape(SHELLS * HALVES, NLAT)
        forcing = lax.dot_general(
            lat, legendre[m], (((1,), (1,)), ((), ())), preferred_element_type=F32
        )
        right_side = field[:, m].reshape(SHELLS * HALVES, DEG) + forcing
        for tile in range(TILES):
            row = (m * TILES + tile) * HALVES
            solved[:, row : row + HALVES, :] = right_side[
                :, tile * LANES : (tile + 1) * LANES
            ].reshape(SHELLS, HALVES, LANES)
    value = solved[0] * pivots[0]
    solved[0] = value
    for i in range(1, SHELLS):
        value = (solved[i] + shell[1, i] * value) * pivots[i]
        solved[i] = value
    ends[1] = value.astype(BF16)
    for i in reversed(range(SHELLS - 1)):
        value = solved[i] + (shell[2, i] * pivots[i]) * value
        solved[i] = value
    ends[0] = value.astype(BF16)


def forcing_solve(me, shell, slots, legendre, field, pivots):
    return pl.pallas_call(
        forcing_kernel,
        out_shape=(
            jax.ShapeDtypeStruct((SHELLS, ROWS, LANES), F32),
            jax.ShapeDtypeStruct((2, ROWS, LANES), BF16),
        ),
        in_specs=[whole(pltpu.SMEM)] * 2 + [whole()] * 3 + [whole(pl.ANY)] * NMODE,
        out_specs=(whole(), whole()),
        scratch_shapes=[
            pltpu.VMEM((SHELLS, PAIRS, NLAT), BF16),
            pltpu.SemaphoreType.DMA((NMODE,)),
        ],
        compiler_params=params(20),
        cost_estimate=cost(2 * 64 * DEG * NLAT * ORD, 16_000_000),
        name="forcing_solve",
    )(me, shell, field, pivots, legendre, *slots)


def chain_values(links, values, first, last):
    alphas = [first]
    for k in range(CHAIN):
        first_value, last_value = values[k]
        alpha = last_value + links(k, 3) * first_value
        if alphas[-1] is not None:
            alpha = alpha + links(k, 4) * alphas[-1]
        alphas.append(alpha)
    firsts = [None] * CHAIN + [last]
    for k in reversed(range(CHAIN)):
        value = links(k, 0) * values[k][0]
        if alphas[k] is not None:
            value = value + links(k, 1) * alphas[k]
        if firsts[k + 1] is not None:
            value = value + links(k, 2) * firsts[k + 1]
        firsts[k] = value
    return alphas, firsts


def boundary_values(links, alphas, firsts, shape):
    zero = jnp.zeros(shape, F32)
    pairs = []
    for k in range(CHAIN):
        before = zero if alphas[k] is None else alphas[k] + links(k, 5) * firsts[k]
        behind = zero if firsts[k + 1] is None else firsts[k + 1]
        pairs.append((before, behind))
    return pairs


def slot_copies(position, slots, held, sems):
    return [
        pltpu.make_async_copy(slot, held.at[lax.rem(position + CHAIN - s, CHAIN)], sems.at[s])
        for s, slot in enumerate(slots)
    ]


def inner_kernel(place, links, a, b, c, d, out, held, coefficients, sems):
    copies = slot_copies(place[1], (a, b, c, d), held, sems)
    copies.append(pltpu.make_async_copy(links, coefficients, sems.at[CHAIN]))
    for copy in copies:
        copy.start()
    for copy in copies:
        copy.wait()
    values = [(held[k, 0].astype(F32), held[k, 1].astype(F32)) for k in range(CHAIN)]
    alphas, firsts = chain_values(lambda k, n: coefficients[k, n], values, None, None)
    out[0] = firsts[0].astype(BF16)
    out[1] = alphas[CHAIN].astype(BF16)


def inner_join(place, links, slots):
    return pl.pallas_call(
        inner_kernel,
        out_shape=jax.ShapeDtypeStruct((2, ROWS, LANES), BF16),
        in_specs=[whole(pltpu.SMEM)] + [whole(pl.ANY)] * 5,
        out_specs=whole(),
        scratch_shapes=[
            pltpu.VMEM((CHAIN, 2, ROWS, LANES), BF16),
            pltpu.VMEM((CHAIN, 6, ROWS, LANES), F32),
            pltpu.SemaphoreType.DMA((CHAIN + 1,)),
        ],
        compiler_params=params(12),
        cost_estimate=cost(1_000_000, 2_000_000),
        name="inner_join",
    )(place, links, *slots)


PIECES = 4
PIECE = SHELLS // PIECES


def final_kernel(place, inner, outer, a, b, c, d, e, f, g, h, solved, left, right, out, *scratch):
    near, far, near_links, far_links, pairs, terms, result, sems, term_sems, out_sems = scratch
    copies = slot_copies(place[0], (e, f, g, h), far, sems.at[0])
    copies.append(pltpu.make_async_copy(outer, far_links, sems.at[0, CHAIN]))
    copies += slot_copies(place[1], (a, b, c, d), near, sems.at[1])
    copies.append(pltpu.make_async_copy(inner, near_links, sems.at[1, CHAIN]))
    term_copies = [
        pltpu.make_async_copy(source, terms.at[n], term_sems.at[n])
        for n, source in enumerate((solved, left, right))
    ]
    for copy in copies + term_copies:
        copy.start()
    for copy in copies:
        copy.wait()
    first = last = None
    for level, (held, links) in enumerate(((far, far_links), (near, near_links))):
        values = [(held[k, 0].astype(F32), held[k, 1].astype(F32)) for k in range(CHAIN)]
        read = lambda k, n, links=links: links[k, n]
        alphas, firsts = chain_values(read, values, first, last)
        found = boundary_values(read, alphas, firsts, (ROWS, LANES))
        for k, (before, behind) in enumerate(found):
            pairs[k, 0] = before
            pairs[k, 1] = behind
        first, last = pairs[place[level], 0], pairs[place[level], 1]
    for copy in term_copies:
        copy.wait()
    sent = []
    for piece in range(PIECES):
        for i in range(piece * PIECE, (piece + 1) * PIECE):
            value = terms[0, i] + terms[1, i] * first + terms[2, i] * last
            value = value.reshape(ORD, TILES, HALVES, LANES)
            for tile in range(TILES):
                result[i, :, :, tile * LANES : (tile + 1) * LANES] = value[:, tile]
        here = pl.ds(piece * PIECE, PIECE)
        sent.append(pltpu.make_async_copy(result.at[here], out.at[here], out_sems.at[piece]))
        sent[-1].start()
    for copy in sent:
        copy.wait()


def final_join(place, inner, outer, slots, super_slots, solved, left, right):
    return pl.pallas_call(
        final_kernel,
        out_shape=jax.ShapeDtypeStruct((SHELLS, ORD, HALVES, DEG), F32),
        in_specs=[whole(pltpu.SMEM)] + [whole(pl.ANY)] * 13,
        out_specs=whole(pl.ANY),
        scratch_shapes=[
            pltpu.VMEM((CHAIN, 2, ROWS, LANES), BF16),
            pltpu.VMEM((CHAIN, 2, ROWS, LANES), BF16),
            pltpu.VMEM((CHAIN, 6, ROWS, LANES), F32),
            pltpu.VMEM((CHAIN, 6, ROWS, LANES), F32),
            pltpu.VMEM((CHAIN, 2, ROWS, LANES), F32),
            pltpu.VMEM((3, SHELLS, ROWS, LANES), F32),
            pltpu.VMEM((SHELLS, ORD, HALVES, DEG), F32),
            pltpu.SemaphoreType.DMA((2, CHAIN + 1)),
            pltpu.SemaphoreType.DMA((3,)),
            pltpu.SemaphoreType.DMA((PIECES,)),
        ],
        compiler_params=params(24),
        cost_estimate=cost(3_000_000, 9_000_000),
        name="final_join",
    )(place, inner, outer, *slots, *super_slots, solved, left, right)


def shifted(array, axis, step):
    size = lax.axis_size(axis)
    return lax.ppermute(array, axis, [(i, (i + step) % size) for i in range(size)])


def ring(array, axis):
    return [array] + [shifted(array, axis, step) for step in range(1, CHAIN)]


def on_device(scalar_field, radial_flow, legendre, diffusivity):
    synth, analysis = (jnp.asarray(table) for table in longitude_tables(ORD * NMODE))
    mode = lax.axis_index(MODE).astype(jnp.int32)
    me = mode.reshape(1)
    firsts = list(synthesis(0, me, scalar_field, radial_flow, legendre))
    later, firsts[0] = lax.optimization_barrier((me, firsts[0]))
    seconds = synthesis(1, later, scalar_field, radial_flow, legendre)
    firsts, seconds = moved_all(firsts, False), moved_all(seconds, False)
    diffusivity, mode, firsts[4] = lax.optimization_barrier((diffusivity, mode, firsts[4]))

    nr_total = SHELLS * CHAIN * CHAIN
    place = jnp.stack([lax.axis_index(RADIAL[0]), lax.axis_index(RADIAL[1])]).astype(jnp.int32)
    shell_ids = lax.axis_index(RADIAL) * SHELLS + jnp.arange(SHELLS, dtype=jnp.int32)
    radius = (nr_total * 7 // 13 + shell_ids).astype(F32)
    shell = jnp.stack(
        [
            diffusivity,
            jnp.where(shell_ids > 0, diffusivity, 0.0),
            jnp.where(shell_ids < nr_total - 1, diffusivity, 0.0),
            radius * radius,
        ]
    )
    row = np.arange(ROWS)[:, None]
    local_degree = row // (TILES * HALVES) + row // HALVES % TILES * LANES + np.arange(LANES)[None]
    degree = (local_degree + mode * ORD).astype(F32)
    angular = degree * (degree + 1.0)
    pivots, left, right = block_matrix(shell, angular)
    near = jnp.concatenate(ring(diffusivity.reshape(1, SHELLS), RADIAL[1]))
    blocks = ring(near, RADIAL[0])
    inner, outer = levels(jnp.concatenate([place, mode.reshape(1)]), blocks)

    modes = moved_all(grid_product(me, synth, analysis, firsts, seconds), True)
    pivots, inner, outer = lax.optimization_barrier((pivots, inner, outer))
    solved, own = forcing_solve(me, shell, modes, legendre, scalar_field, pivots)
    slots = ring(own, RADIAL[1])
    super_slots = ring(inner_join(place, inner, slots), RADIAL[0])
    return final_join(place, inner, outer, slots, super_slots, solved, left, right)


def solution(mesh):
    finer = Mesh(
        mesh.devices.reshape(4, 4, 4, 2), ("radial_0", "radial_1", "mode_0", "mode_1")
    )
    return jax.shard_map(
        on_device,
        mesh=finer,
        in_specs=(
            P(RADIAL, MODE, None, None),
            P(RADIAL, MODE, None, None),
            P(MODE, None, None),
            P(RADIAL),
        ),
        out_specs=P(RADIAL, MODE, None, None),
        check_vma=False,
    )
```
